512 devices in a mesh: leaf: 128 (over y, z, core), rep: 4 (over x).
Axes of the slice: x: 4, y: 8, z: 8, core: 2. Of those that a mesh axis runs over, the one named last changes fastest.
Arguments:
- bottom_factor: float32 [512, 4096], P('leaf'), may hold values from -1 to 3, as said below
- transfer0: float32 [512, 4096], P('leaf'), may hold values from -0.3 to 1, as said below
- transfer1: float32 [256, 4096], P('leaf'), may hold values from -0.3 to 1, as said below
- transfer2: float32 [128, 4096], P('leaf'), may hold values from -0.3 to 1, as said below
- transfer3: float32 [64, 4096], replicated, may hold values from -0.3 to 1, as said below
- child_order: int32 [128, 4], P('leaf'), may hold values from 0 to 3, each once within a row
- coupling: bfloat16 [98304, 4096], P(('leaf', 'rep')), may hold values from -4 to 4
- admissible: int32 [3, 98304], P(None, ('leaf', 'rep')), may hold values from 0 to 511, as said below
Outputs:
- projected: bfloat16 [98304, 4096], P(('leaf', 'rep'))
- gram0: float32 [512, 4096], P('leaf')
- gram1: float32 [256, 4096], P('leaf')
- gram2: float32 [128, 4096], P('leaf')
The draws below stay inside these ranges and needn't reach their ends.
Inputs may be any that keep to these rules, and one draw needn't show every extreme that they name: `bottom_factor`: each row is an upper-triangular 64 x 64 matrix with positive diagonal. `transfer0`: rows are 64 x 64 matrices. `transfer1`: rows are 64 x 64 matrices. `transfer2`: rows are 64 x 64 matrices. `transfer3`: rows are 64 x 64 matrices. `admissible`: entry (0, b) is a level 0 to 4. With l = b // (192 times the size of rep): entry (1, b) is a cluster of that level numbered from 0, at levels 0 to 2 one of the 4 / 2^level clusters starting at l * 4 / 2^level, at level 3 cluster l // 2, at level 4 cluster l // 4; entry (2, b) at levels 0 to 2 is another cluster of that level held in the same way by leaf index l - 1, l or l + 1, at levels 3 and 4 the row cluster's sibling (its number XOR 1).
All inputs are finite; a program needn't handle non-finite values.
Results may differ from the reference program's by a relative error of at most 0.0064.
Values may be sent and summed in bfloat16 or wider, within the bound.
A program may use at most 64 MiB of HBM per device.

```python
import jax
import jax.numpy as jnp
from jax import lax

RANK = 64
CL_DEV = 4
BLK_DEV = 192
LEVEL2 = 128
BLOCKS = 98304
N_LEAF = 128
N_REP = 4


def assemble_transfer(jitter):
    unit_matrix = jnp.eye(RANK, dtype=jnp.float32)
    return (0.7 * unit_matrix[None] + jitter).reshape(jitter.shape[0], RANK * RANK)


def transfer_jitter_normal(key, count):
    return jax.random.truncated_normal(key, -3.0, 3.0, (count, RANK, RANK), jnp.float32) * (0.35 * RANK ** (-0.5))


def draw_transfer0(key, part):
    key = jax.random.fold_in(key, 11)
    return assemble_transfer(transfer_jitter_normal(key, CL_DEV * N_LEAF))


def draw_transfer1(key, part):
    key = jax.random.fold_in(key, 12)
    return assemble_transfer(transfer_jitter_normal(key, CL_DEV * N_LEAF // 2))


def draw_transfer2(key, part):
    key = jax.random.fold_in(key, 13)
    return assemble_transfer(transfer_jitter_normal(key, CL_DEV * N_LEAF // 4))


def draw_transfer3(key, part):
    key = jax.random.fold_in(key, 14)
    return assemble_transfer(transfer_jitter_normal(key, CL_DEV * N_LEAF // 8))


def draw_bottom_factor(key, part):
    key = jax.random.fold_in(key, 3)
    first_key, second_key = jax.random.split(key)
    count = CL_DEV * N_LEAF
    diagonal = jax.random.uniform(first_key, (count, RANK), jnp.float32, 1.0, 2.0)
    upper_part = jax.random.truncated_normal(second_key, -3.0, 3.0, (count, RANK, RANK), jnp.float32) * 0.3
    row_index = lax.broadcasted_iota(jnp.int32, (RANK, RANK), 0)
    column_index = lax.broadcasted_iota(jnp.int32, (RANK, RANK), 1)
    strict_upper = (row_index < column_index).astype(jnp.float32)
    unit_matrix = (row_index == column_index).astype(jnp.float32)
    result = diagonal[:, :, None] * unit_matrix[None] + upper_part * strict_upper[None]
    return result.reshape(count, RANK * RANK)


def draw_admissible(key, part):
    key = jax.random.fold_in(key, 7)
    keys = jax.random.split(key, 4)
    count = BLK_DEV * N_LEAF * N_REP
    bucket = jax.random.randint(keys[0], (count,), 0, 16, dtype=jnp.int32)
    level = (bucket >= 8).astype(jnp.int32) + (bucket >= 12).astype(jnp.int32) + (bucket >= 14).astype(jnp.int32) + (bucket >= 15).astype(jnp.int32)
    owner = jnp.arange(count, dtype=jnp.int32) // (BLK_DEV * N_REP)
    per_leaf = jnp.maximum(CL_DEV // jnp.left_shift(1, level), 1)
    level_count = CL_DEV * N_LEAF // jnp.left_shift(1, level)
    row_low = owner * per_leaf + jax.random.randint(keys[1], (count,), 0, 1024, dtype=jnp.int32) % per_leaf
    neighbour_step = jax.random.randint(keys[2], (count,), 0, 3, dtype=jnp.int32) - 1
    neighbour = owner + neighbour_step
    neighbour = jnp.where((neighbour < 0) | (neighbour >= N_LEAF), owner, neighbour)
    column_low = neighbour * per_leaf + jax.random.randint(keys[3], (count,), 0, 1024, dtype=jnp.int32) % per_leaf
    column_low = jnp.where(column_low == row_low, jnp.where(row_low + per_leaf < level_count, row_low + per_leaf, row_low - per_leaf), column_low)
    row_high = jnp.right_shift(owner, jnp.maximum(level - 2, 0))
    column_high = jnp.bitwise_xor(row_high, 1)
    rows = jnp.where(level <= 2, row_low, row_high)
    columns = jnp.where(level <= 2, column_low, column_high)
    return jnp.stack([level, rows, columns]).astype(jnp.int32)


def level_of(key, extent, cuts, smallest, largest):
    def one(position, parts):
        steps = jax.random.uniform(jax.random.fold_in(jax.random.fold_in(key, 6), position), (parts,), jnp.float32, smallest / len(cuts), largest / len(cuts))
        return jnp.repeat(jnp.exp(steps), extent[position] // parts).reshape((-1,) + (1,) * (len(extent) - position - 1))

    gain = one(*cuts[0])
    for cut in cuts[1:]:
        gain = gain * one(*cut)
    return gain


def gaussian(rng, extent, deviation, most, cuts=(), kind=jnp.bfloat16):
    gain = level_of(rng, extent, cuts, -0.22, 0.18) if cuts else 1.0
    values = jax.random.normal(rng, extent, jnp.float32) * deviation * gain
    return jnp.minimum(jnp.maximum(values, -most), most).astype(kind)


def setup_inputs(seed: int = 0) -> dict:
    seeds = jax.random.split(jax.random.key(seed), 9)
    bottom_factor = draw_bottom_factor(jax.random.fold_in(seeds[8], 71), 0)
    transfer0 = draw_transfer0(jax.random.fold_in(seeds[8], 71), 0)
    transfer1 = draw_transfer1(jax.random.fold_in(seeds[8], 71), 0)
    transfer2 = draw_transfer2(jax.random.fold_in(seeds[8], 71), 0)
    transfer3 = draw_transfer3(jax.random.fold_in(seeds[8], 71), 0)
    child_order = jax.vmap(lambda own: jax.random.permutation(own, CL_DEV))(jax.random.split(seeds[5], LEVEL2)).reshape((LEVEL2, CL_DEV)).astype(jnp.int32)
    coupling = gaussian(seeds[6], (BLOCKS, RANK * RANK), 0.25, 4.0, ((0, 512),))
    admissible = draw_admissible(jax.random.fold_in(seeds[8], 71), 0)
    return {"bottom_factor": bottom_factor, "transfer0": transfer0, "transfer1": transfer1, "transfer2": transfer2, "transfer3": transfer3, "child_order": child_order, "coupling": coupling, "admissible": admissible}


HIGHEST_PRECISION = lax.Precision.HIGHEST

def squares(flat):
    return flat.reshape(-1, RANK, RANK)

def apply_transfer(factors, transfers):
    return jnp.einsum('cij,cjk->cik', factors, transfers, precision=HIGHEST_PRECISION)

def upper_factor(gram):
    lower = jnp.linalg.cholesky(gram)
    return jnp.swapaxes(lower, 1, 2)

def merge_pair(first_kid, second_kid):
    gram = jnp.einsum('cki,ckj->cij', first_kid, first_kid, precision=HIGHEST_PRECISION)
    gram = gram + jnp.einsum('cki,ckj->cij', second_kid, second_kid, precision=HIGHEST_PRECISION)
    return upper_factor(gram)

def reference(bottom_factor, transfer0, transfer1, transfer2, transfer3, child_order, coupling, admissible):
    clusters = CL_DEV * N_LEAF
    level_zero = squares(bottom_factor)
    images_zero = apply_transfer(level_zero, squares(transfer0))
    children = (CL_DEV * jnp.arange(N_LEAF, dtype=jnp.int32)[:, None] + child_order).reshape(-1)
    level_one = merge_pair(images_zero[children[0::2]], images_zero[children[1::2]])
    images_one = apply_transfer(level_one, squares(transfer1))
    level_two = merge_pair(images_one[0::2], images_one[1::2])
    images_two = apply_transfer(level_two, squares(transfer2))
    level_three = merge_pair(images_two[0::2], images_two[1::2])
    images_three = apply_transfer(level_three, squares(transfer3))
    level_four = merge_pair(images_three[0::2], images_three[1::2])
    factor_table = jnp.concatenate([level_zero, level_one, level_two, level_three, level_four]).astype(jnp.bfloat16)
    starts = jnp.array([0, clusters, clusters + clusters // 2, clusters + 3 * clusters // 4, clusters + 7 * clusters // 8], dtype=jnp.int32)
    levels = admissible[0]
    row_ids = starts[levels] + admissible[1]
    column_ids = starts[levels] + admissible[2]
    lower_count = clusters + clusters // 2 + clusters // 4
    gram_index = jnp.where(levels <= 2, row_ids, lower_count).astype(jnp.int32)
    groups = N_LEAF * N_REP

    def one_group(carry, inputs):
        rows_here, columns_here, grams_here, blocks = inputs
        row_factors = factor_table[rows_here].astype(jnp.float32)
        column_factors = factor_table[columns_here].astype(jnp.float32)
        block_mats = blocks.astype(jnp.float32).reshape(-1, RANK, RANK)
        half_product = jnp.einsum('bij,bjk->bik', row_factors, block_mats, precision=HIGHEST_PRECISION).astype(jnp.bfloat16)
        result = jnp.einsum('bik,blk->bil', half_product.astype(jnp.float32), column_factors, precision=HIGHEST_PRECISION)
        gram_terms = jnp.einsum('bil,bml->bim', result, result, precision=HIGHEST_PRECISION) / RANK
        carry = carry.at[grams_here].add(gram_terms.reshape(-1, RANK * RANK), mode='drop')
        return (carry, result.astype(jnp.bfloat16).reshape(-1, RANK * RANK))
    initial = jnp.zeros((lower_count, RANK * RANK), jnp.float32)
    grams, projected = lax.scan(one_group, initial, (row_ids.reshape(groups, -1), column_ids.reshape(groups, -1), gram_index.reshape(groups, -1), coupling.reshape(groups, -1, RANK * RANK)))
    return (projected.reshape(-1, RANK * RANK), grams[:clusters], grams[clusters:clusters + clusters // 2], grams[clusters + clusters // 2:])
```

```python
import functools

import jax
import jax.numpy as jnp
from jax import lax
from jax.experimental import pallas as pl
from jax.experimental.pallas import tpu as pltpu
from jax.sharding import PartitionSpec as P

RANK = 64
HALF = 32
LANES = 128
FLAT = RANK * RANK
CL_DEV = 4
SLOTS = 7
ROW_SLOTS = 9
COLUMNS = 3 * SLOTS + 2
GROUP = 8
MESH = pl.DeviceIdType.MESH
F32 = jnp.float32
BF16 = jnp.bfloat16
EXACT = lax.Precision.HIGHEST
MIB = 1024 * 1024


def lanes_left(rows):
    return lax.broadcasted_iota(jnp.int32, (rows, LANES), 1) < RANK


def swap(x):
    return pltpu.roll(x, RANK, 1)


def exact_dot(a, b):
    return jnp.dot(a, b, precision=EXACT, preferred_element_type=F32)


def exact_gram(a, b):
    return lax.dot_general(a, b, (((0,), (0,)), ((), ())), precision=EXACT, preferred_element_type=F32)


def flipped(index, bits):
    result = index
    for place in range(3):
        if bits >> place & 1:
            result = result + (1 - 2 * (index // (1 << place) % 2)) * (1 << place)
    return result


def tiles_of(flat, rows, lines):
    for tile in range(HALF):
        lines[tile * 8 : tile * 8 + rows, :] = flat[:, tile * LANES : (tile + 1) * LANES]


def packed(lines, which):
    return lines[pl.ds(which, HALF, stride=8), :]


def natural_pair(left, right, page):
    side = lanes_left(HALF)
    page[pl.ds(0, HALF, stride=2), :] = jnp.where(side, left, swap(right))
    page[pl.ds(1, HALF, stride=2), :] = jnp.where(side, swap(left), right)
    return page[...]


def pack(x):
    return jnp.concatenate([x[:HALF], x[HALF:]], axis=1)


def unpack(x):
    return jnp.concatenate([x[:, :RANK], x[:, RANK:]], axis=0)


def upsweep_kernel(
    leaves, chunk,
    order, bottom, zero, one, two, three,
    grams_out, factors_out,
    lines, lines_three, flat_three, page, kids, factors, pairs, tops, images,
    three_sem, send, receive,
):
    me = lax.axis_index("leaf")
    rep = lax.axis_index("rep")
    left = lax.rem(me + leaves - 1, leaves)
    right = lax.rem(me + 1, leaves)
    others = [flipped(me, bits) for bits in range(1, GROUP)]
    barrier = pltpu.get_barrier_semaphore()
    for other in [left, right] + others:
        pl.semaphore_signal(barrier, inc=1, device_id=(other, rep), device_id_type=MESH)
    start = pl.multiple_of(me // 2 // chunk * chunk, chunk)
    fetch = pltpu.make_async_copy(three.at[pl.ds(start, chunk)], flat_three, three_sem)
    fetch.start()

    tiles_of(bottom, CL_DEV, lines)
    bottoms = [packed(lines, c) for c in range(CL_DEV)]
    leaf_pairs = [natural_pair(bottoms[c], bottoms[c + 1], page) for c in (0, 2)]
    for k in range(2):
        factors[1, k * RANK : (k + 1) * RANK, :] = leaf_pairs[k].astype(BF16)
    tiles_of(zero, CL_DEV, lines)
    zeros = [packed(lines, c) for c in range(CL_DEV)]
    zero_pairs = [natural_pair(zeros[c], zeros[c + 1], page) for c in (0, 2)]
    tiles_of(one, CL_DEV // 2, lines)
    ones = natural_pair(packed(lines, 0), packed(lines, 1), page)
    tiles_of(two, 1, lines)
    own_two = packed(lines, 0)
    twos = natural_pair(own_two, own_two, page)[:, :RANK]

    for c in range(CL_DEV):
        half = slice(c % 2 * RANK, c % 2 * RANK + RANK)
        image = exact_dot(leaf_pairs[c // 2][:, half], zero_pairs[c // 2][:, half])
        kids[c] = exact_gram(image, image)
    level_one = [kids[order[0, 2 * i]] + kids[order[0, 2 * i + 1]] for i in range(2)]
    pairs[1, :RANK, :] = jnp.concatenate(level_one, axis=1)
    level_two = 0.0
    for i in range(2):
        transfer = ones[:, i * RANK : (i + 1) * RANK]
        level_two = level_two + exact_gram(transfer, exact_dot(level_one[i], transfer))
    pairs[1, RANK:, :] = pack(level_two)
    tops[0] = pack(exact_gram(twos, exact_dot(level_two, twos)))

    pl.semaphore_wait(barrier, GROUP + 1)
    copies = []

    def push(source, target, device):
        place = len(copies)
        copy = pltpu.make_async_remote_copy(
            src_ref=source, dst_ref=target, send_sem=send.at[place], recv_sem=receive.at[place],
            device_id=(device, rep), device_id_type=MESH,
        )
        copy.start()
        copies.append(copy)

    for bits in range(1, GROUP):
        push(tops.at[0], tops.at[bits], others[bits - 1])
    push(pairs.at[1], pairs.at[2], left)
    push(pairs.at[1], pairs.at[0], right)
    push(factors.at[1], factors.at[2], left)
    push(factors.at[1], factors.at[0], right)

    fetch.wait()
    tiles_of(flat_three, chunk, lines_three)
    place = lax.rem(me // 2, chunk)
    threes = []
    for u in range(GROUP // 2):
        own = packed(lines_three, flipped(place, u))
        threes.append(natural_pair(own, own, page)[:, :RANK])
    for copy in copies[: GROUP - 1]:
        copy.wait_recv()
    level_three, lifted = [], []
    for u in range(GROUP // 2):
        gram = unpack(tops[2 * u] + tops[2 * u + 1])
        level_three.append(gram)
        lifted.append(exact_gram(threes[u], exact_dot(gram, threes[u])))
    level_four = [lifted[0] + lifted[1], lifted[2] + lifted[3]]
    for copy in copies[GROUP - 1 :]:
        copy.wait_recv()
    for side in range(3):
        grams_out[side * RANK : (side + 1) * RANK, :] = pairs[side, :RANK, :]
        factors_out[side * LANES : (side + 1) * LANES, :] = factors[side]
    side_two = [unpack(pairs[side, RANK:, :]) for side in range(3)]
    rest = side_two + [level_three[0], level_three[1], level_four[0], level_four[1], level_four[1]]
    for k in range(4):
        at = (3 + k) * RANK
        grams_out[at : at + RANK, :] = jnp.concatenate([rest[2 * k], rest[2 * k + 1]], axis=1)
    grams_out[7 * RANK :, :] = pairs[1, :RANK, :]
    for copy in copies:
        copy.wait_send()


def upsweep(leaves, order, bottom, zero, one, two, three):
    chunk = min(8, three.shape[0])
    vmem = pl.BlockSpec(memory_space=pltpu.VMEM)
    count = GROUP + 3
    return pl.pallas_call(
        functools.partial(upsweep_kernel, leaves, chunk),
        out_shape=[
            jax.ShapeDtypeStruct((8 * RANK, LANES), F32),
            jax.ShapeDtypeStruct((3 * LANES, LANES), BF16),
        ],
        in_specs=[pl.BlockSpec(memory_space=pltpu.SMEM)] + [vmem] * 4 + [pl.BlockSpec(memory_space=pl.ANY)],
        out_specs=[vmem, vmem],
        scratch_shapes=[
            pltpu.VMEM((HALF * 8, LANES), F32),
            pltpu.VMEM((HALF * 8, LANES), F32),
            pltpu.VMEM((chunk, FLAT), F32),
            pltpu.VMEM((RANK, LANES), F32),
            pltpu.VMEM((CL_DEV, RANK, RANK), F32),
            pltpu.VMEM((3, LANES, LANES), BF16),
            pltpu.VMEM((3, RANK + HALF, LANES), F32),
            pltpu.VMEM((GROUP, HALF, LANES), F32),
            pltpu.VMEM((8, LANES), F32),
            pltpu.SemaphoreType.DMA,
            pltpu.SemaphoreType.DMA((count,)),
            pltpu.SemaphoreType.DMA((count,)),
        ],
        compiler_params=pltpu.CompilerParams(
            collective_id=0, has_side_effects=True, vmem_limit_bytes=32 * MIB
        ),
        name="upsweep",
    )(order, bottom, zero, one, two, three)


def picked(x, index):
    return jnp.take_along_axis(x, index, axis=1, mode="promise_in_bounds")


def factorize(rows):
    lane = lax.broadcasted_iota(jnp.int32, (8, LANES), 1)
    base = jnp.where(lane < RANK, 0, RANK)
    inner = lane - base
    rows = list(rows)
    result = []
    for panel in range(0, RANK, 8):
        entry = {}
        for r in range(8):
            for c in range(r, 8):
                entry[r, c] = picked(rows[panel + r], base + (panel + c))
        done = []
        for k in range(8):
            scale = lax.rsqrt(entry[k, k])
            done.append(rows[panel + k] * scale)
            for c in range(k + 1, 8):
                entry[k, c] = entry[k, c] * scale
            for r in range(k + 1, 8):
                rows[panel + r] = rows[panel + r] - entry[k, r] * done[k]
                for c in range(r, 8):
                    entry[r, c] = entry[r, c] - entry[k, r] * entry[k, c]
        for i in range(panel + 8, RANK):
            for k in range(8):
                rows[i] = rows[i] - picked(done[k], base + i) * done[k]
        for k in range(8):
            result.append(jnp.where(inner >= panel + k, done[k], 0.0))
    return result


def visit_order(admissible, leaf, padded_in):
    wide = 256
    padded_in[...] = jnp.full(padded_in.shape, -1, jnp.int32)
    padded_in[0:3, 0 : admissible.shape[1]] = admissible[...]
    level = padded_in[0:1, :]
    row = padded_in[1:2, :]
    column = padded_in[2:3, :]
    low = level <= 2
    base = jnp.where(level == 0, 0, jnp.where(level == 1, CL_DEV, CL_DEV + CL_DEV // 2))
    shift = jnp.where(level == 0, 2, jnp.where(level == 1, 1, 0))
    held = jnp.left_shift(1, shift) - 1
    slot = jnp.where(low, base + jnp.bitwise_and(row, held), level + (SLOTS - 3))
    slot = jnp.where(level < 0, -1, slot)
    side = jnp.clip(jnp.right_shift(column, shift) - leaf + 1, 0, 2)
    place = jnp.where(
        low, side * SLOTS + base + jnp.bitwise_and(column, held), 3 * SLOTS + level - 3
    )
    member = lax.broadcasted_iota(jnp.int32, (16, wide), 0) == slot
    ahead = lax.broadcasted_iota(jnp.int32, (wide, wide), 0) <= lax.broadcasted_iota(
        jnp.int32, (wide, wide), 1
    )
    member_f = jnp.where(member, 1.0, 0.0).astype(F32)
    rank = jnp.dot(member_f.astype(BF16), jnp.where(ahead, 1.0, 0.0).astype(BF16), preferred_element_type=F32)
    count = jnp.sum(member_f, axis=1, keepdims=True)
    even = jnp.floor((count + 1.0) * 0.5) * 2.0
    even = jnp.broadcast_to(even, (16, wide)).astype(BF16)
    below = lax.broadcasted_iota(jnp.int32, (16, 16), 1) < lax.broadcasted_iota(jnp.int32, (16, 16), 0)
    begin = jnp.dot(jnp.where(below, 1.0, 0.0).astype(BF16), even, preferred_element_type=F32)
    at = jnp.sum(jnp.where(member, begin + rank - 1.0, 0.0), axis=0, keepdims=True)
    at = jnp.where(slot < 0, -1.0, at).astype(jnp.int32)
    chosen = lax.broadcasted_iota(jnp.int32, (wide, wide), 0) == at
    line = lax.broadcasted_iota(jnp.int32, (8, wide), 0)
    number = lax.broadcasted_iota(jnp.int32, (8, wide), 1) + 1
    values = jnp.where(line == 0, number, jnp.where(line == 1, place, jnp.where(line == 2, slot, 0)))
    return lax.dot_general(
        values.astype(F32).astype(BF16), jnp.where(chosen, 1.0, 0.0).astype(BF16),
        (((1,), (1,)), ((), ())), preferred_element_type=F32,
    ).astype(jnp.int32)


def blocks_kernel(
    blocks, pairs,
    admissible, grams, leaf_factors, coupling,
    projected, weights_out,
    padded_in, order_v, order, lines, upper, row_table, column_left, column_right,
    own, turned, results, totals, order_sem,
):
    leaf = lax.axis_index("leaf")
    side = lanes_left(HALF)
    side_full = lanes_left(RANK)
    lane = lax.broadcasted_iota(jnp.int32, (RANK, LANES), 1)
    inner = jnp.where(lane < RANK, lane, lane - RANK)
    spread = jnp.where(inner < HALF, 2 * inner, 2 * inner - (RANK - 1)) + (lane - inner)

    order_v[...] = visit_order(admissible, leaf, padded_in)
    to_scalar = pltpu.make_async_copy(order_v, order, order_sem)
    to_scalar.start()

    own[0] = jnp.zeros((HALF, LANES), BF16)
    turned[0] = jnp.zeros((HALF, LANES), BF16)

    def lay(group, carry):
        first = pl.multiple_of(group * 16, 16)
        x = coupling[pl.ds(first, 16), :].astype(F32)
        for h in range(2):
            for tile in range(HALF):
                at = (h * HALF + tile) * 8
                lines[at : at + 8, :] = x[8 * h : 8 * h + 8, tile * LANES : (tile + 1) * LANES]
        for s in range(16):
            block = lines[pl.ds(s // 8 * 256 + s % 8, HALF, stride=8), :]
            own[first + s + 1] = block.astype(BF16)
            turned[first + s + 1] = swap(block).astype(BF16)
        return carry

    lax.fori_loop(0, blocks // 16, lay, 0)

    rows = factorize([grams[pl.ds(i, 8, stride=RANK), :] for i in range(RANK)])
    for i in range(RANK):
        upper[i * 8 : (i + 1) * 8, :] = rows[i]

    def put_column(where, left, right):
        column_left[where] = left.astype(BF16)
        column_right[where] = right.astype(BF16)

    def put_columns(first, second, names):
        flipped_all = jnp.transpose(jnp.concatenate([first, second], axis=0))
        for half in range(2):
            part = flipped_all[half * RANK : (half + 1) * RANK]
            other = swap(part)
            if names[half] is not None:
                put_column(names[half], jnp.where(side_full, part, 0.0), jnp.where(side_full, 0.0, other))
            if names[2 + half] is not None:
                put_column(names[2 + half], jnp.where(side_full, other, 0.0), jnp.where(side_full, 0.0, part))

    def put_rows(even, odd, names):
        x = picked(jnp.concatenate([even, odd], axis=0), spread)
        if names[0] is not None:
            row_table[names[0]] = x.astype(BF16)
        if names[1] is not None:
            row_table[names[1]] = swap(x).astype(BF16)

    for near in range(3):
        first = leaf_factors[near * LANES : near * LANES + RANK, :].astype(F32)
        second = leaf_factors[near * LANES + RANK : (near + 1) * LANES, :].astype(F32)
        put_columns(first, second, [near * SLOTS + c for c in (0, 1, 2, 3)])
        if near == 1:
            for k, x in enumerate((first, second)):
                lines[k * RANK : (k + 1) * RANK, :] = x
                put_rows(
                    lines[pl.ds(k * RANK, HALF, stride=2), :],
                    lines[pl.ds(k * RANK + 1, HALF, stride=2), :],
                    (2 * k, 2 * k + 1),
                )
    column_names = [
        (4, 5), (SLOTS + 4, SLOTS + 5), (2 * SLOTS + 4, 2 * SLOTS + 5), (6, SLOTS + 6),
        (2 * SLOTS + 6, None), (3 * SLOTS, None), (3 * SLOTS + 1, None), (None, None),
    ]
    for k in range(0, 8, 2):
        put_columns(
            upper[pl.ds(k, RANK, stride=8), :], upper[pl.ds(k + 1, RANK, stride=8), :],
            column_names[k] + column_names[k + 1],
        )
    for k, names in ((1, (4, 5)), (3, (None, 6)), (4, (None, 7)), (5, (None, 8))):
        put_rows(upper[pl.ds(k, HALF, stride=16), :], upper[pl.ds(8 + k, HALF, stride=16), :], names)

    totals[...] = jnp.zeros(totals.shape, F32)
    to_scalar.wait()

    def visit(pair):
        a, b = order[0, 2 * pair], order[0, 2 * pair + 1]
        slot = order[2, 2 * pair]
        both = jnp.concatenate(
            [jnp.where(side, own[a], turned[b]), jnp.where(side, turned[a], own[b])], axis=0
        )
        half = jnp.dot(row_table[slot][:, :RANK], both, preferred_element_type=F32).astype(BF16)
        columns = jnp.concatenate(
            [column_left[order[1, 2 * pair]], column_right[order[1, 2 * pair + 1]]], axis=0
        )
        result = jnp.dot(half, columns, preferred_element_type=F32)
        rounded = result.astype(BF16)
        totals[slot, :, :RANK] += lax.dot_general(
            rounded, rounded, (((1,), (1,)), ((), ())), preferred_element_type=F32
        )
        top, bottom = result[:HALF], result[HALF:]
        results[pl.ds(pl.multiple_of(a * HALF, HALF), HALF), :] = jnp.where(side, top, swap(bottom))
        results[pl.ds(pl.multiple_of(b * HALF, HALF), HALF), :] = jnp.where(side, swap(top), bottom)

    def visits(step, carry):
        for k in range(4):
            visit(step * 4 + k)
        return carry

    lax.fori_loop(0, pairs // 4, visits, 0)

    gather = jnp.where(inner % 2 == 0, inner // 2, HALF + inner // 2)
    for s in range(SLOTS):
        x = picked(totals[s], gather)
        weights_out[s * HALF : (s + 1) * HALF, :] = jnp.where(side, x[:HALF], x[HALF:]) * (1.0 / RANK)

    def write(group, carry):
        first = pl.multiple_of(group * 16, 16)
        for tile in range(HALF):
            at = (first + 1) * HALF + tile
            x = jnp.concatenate(
                [
                    results[pl.ds(at, 8, stride=HALF), :],
                    results[pl.ds(at + 8 * HALF, 8, stride=HALF), :],
                ],
                axis=0,
            )
            projected[pl.ds(first, 16), tile * LANES : (tile + 1) * LANES] = x.astype(BF16)
        return carry

    lax.fori_loop(0, blocks // 16, write, 0)


def blocks_call(admissible, grams, leaf_factors, coupling):
    blocks = coupling.shape[0]
    pairs = -(-(blocks + ROW_SLOTS) // 2)
    pairs = -(-pairs // 4) * 4
    vmem = pl.BlockSpec(memory_space=pltpu.VMEM)
    return pl.pallas_call(
        functools.partial(blocks_kernel, blocks, pairs),
        out_shape=[
            jax.ShapeDtypeStruct((blocks, FLAT), BF16),
            jax.ShapeDtypeStruct((SLOTS * HALF, LANES), F32),
        ],
        in_specs=[vmem] * 4,
        out_specs=[vmem] * 2,
        scratch_shapes=[
            pltpu.VMEM((8, 256), jnp.int32),
            pltpu.VMEM((8, 256), jnp.int32),
            pltpu.SMEM((8, 256), jnp.int32),
            pltpu.VMEM((512, LANES), F32),
            pltpu.VMEM((512, LANES), F32),
            pltpu.VMEM((ROW_SLOTS, RANK, LANES), BF16),
            pltpu.VMEM((COLUMNS, RANK, LANES), BF16),
            pltpu.VMEM((COLUMNS, RANK, LANES), BF16),
            pltpu.VMEM((blocks + 1, HALF, LANES), BF16),
            pltpu.VMEM((blocks + 1, HALF, LANES), BF16),
            pltpu.VMEM(((blocks + 1) * HALF, LANES), F32),
            pltpu.VMEM((ROW_SLOTS, RANK, LANES), F32),
            pltpu.SemaphoreType.DMA,
        ],
        compiler_params=pltpu.CompilerParams(vmem_limit_bytes=40 * MIB),
        name="blocks",
    )(admissible, grams, leaf_factors, coupling)


def sum_kernel(reps, part, zero, one, two, parts, send, receive):
    leaf = lax.axis_index("leaf")
    me = lax.axis_index("rep")
    barrier = pltpu.get_barrier_semaphore()
    for step in range(1, reps):
        other = lax.rem(me + step, reps)
        pl.semaphore_signal(barrier, inc=1, device_id=(leaf, other), device_id_type=MESH)
    parts[me] = part[...].astype(BF16)
    pl.semaphore_wait(barrier, reps - 1)
    copies = []
    for step in range(1, reps):
        copy = pltpu.make_async_remote_copy(
            src_ref=parts.at[me], dst_ref=parts.at[me],
            send_sem=send.at[step - 1], recv_sem=receive.at[step - 1],
            device_id=(leaf, lax.rem(me + step, reps)), device_id_type=MESH,
        )
        copy.start()
        copies.append(copy)
    for copy in copies:
        copy.wait_recv()
    total = parts[0].astype(F32)
    for k in range(1, reps):
        total = total + parts[k].astype(F32)
    lines = part
    lines[...] = total
    for tile in range(HALF):
        span = slice(tile * LANES, (tile + 1) * LANES)
        zero[:, span] = lines[pl.ds(tile, CL_DEV, stride=HALF), :]
        one[:, span] = lines[pl.ds(tile + CL_DEV * HALF, CL_DEV // 2, stride=HALF), :]
        two[:, span] = lines[tile + (SLOTS - 1) * HALF : tile + (SLOTS - 1) * HALF + 1, :]
    for copy in copies:
        copy.wait_send()


def sum_kernel_outer(reps, part, zero, one, two, lines, parts, send, receive):
    lines[...] = part[...]
    sum_kernel(reps, lines, zero, one, two, parts, send, receive)


def sum_call(reps, part):
    vmem = pl.BlockSpec(memory_space=pltpu.VMEM)
    return pl.pallas_call(
        functools.partial(sum_kernel_outer, reps),
        out_shape=[jax.ShapeDtypeStruct((count, FLAT), F32) for count in (4, 2, 1)],
        in_specs=[vmem],
        out_specs=[vmem] * 3,
        scratch_shapes=[
            pltpu.VMEM(part.shape, F32),
            pltpu.VMEM((reps,) + part.shape, BF16),
            pltpu.SemaphoreType.DMA((reps - 1,)),
            pltpu.SemaphoreType.DMA((reps - 1,)),
        ],
        compiler_params=pltpu.CompilerParams(collective_id=1, has_side_effects=True),
        name="rep_sum",
    )(part)


def local(leaves, reps, bottom, zero, one, two, three, order, coupling, admissible):
    grams, leaf_factors = upsweep(leaves, order, bottom, zero, one, two, three)
    projected, part = blocks_call(admissible, grams, leaf_factors, coupling)
    weights = sum_call(reps, part)
    return projected, *weights


def solution(mesh):
    return jax.shard_map(
        functools.partial(local, mesh.shape["leaf"], mesh.shape["rep"]),
        mesh=mesh,
        in_specs=(
            P("leaf", None),
            P("leaf", None),
            P("leaf", None),
            P("leaf", None),
            P(),
            P("leaf", None),
            P(("leaf", "rep"), None),
            P(None, ("leaf", "rep")),
        ),
        out_specs=(P(("leaf", "rep"), None), P("leaf", None), P("leaf", None), P("leaf", None)),
        check_vma=False,
    )
```

```python
import functools

import jax
import jax.numpy as jnp
from jax import lax
from jax.experimental import pallas as pl
from jax.experimental.pallas import tpu as pltpu
from jax.sharding import PartitionSpec as P

RANK = 64
HALF = 32
LANES = 128
FLAT = RANK * RANK
CL_DEV = 4
SLOTS = 7
ROW_SLOTS = 9
COLUMNS = 3 * SLOTS + 2
GROUP = 8
MESH = pl.DeviceIdType.MESH
F32 = jnp.float32
BF16 = jnp.bfloat16
EXACT = lax.Precision.HIGHEST
WIDE = 256
BATCH = 25
MIB = 1024 * 1024


def lanes_left(rows):
    return lax.broadcasted_iota(jnp.int32, (rows, LANES), 1) < RANK


def swap(x):
    return pltpu.roll(x, RANK, 1)


def exact_dot(a, b):
    return jnp.dot(a, b, precision=EXACT, preferred_element_type=F32)


def exact_gram(a, b):
    return lax.dot_general(a, b, (((0,), (0,)), ((), ())), precision=EXACT, preferred_element_type=F32)


def flipped(index, bits):
    result = index
    for place in range(3):
        if bits >> place & 1:
            result = result + (1 - 2 * (index // (1 << place) % 2)) * (1 << place)
    return result


def tiles_of(flat, rows, lines):
    for tile in range(HALF):
        lines[tile * 8 : tile * 8 + rows, :] = flat[:, tile * LANES : (tile + 1) * LANES]


def packed(lines, which):
    return lines[pl.ds(which, HALF, stride=8), :]


def natural_pair(left, right, page):
    side = lanes_left(HALF)
    page[pl.ds(0, HALF, stride=2), :] = jnp.where(side, left, swap(right))
    page[pl.ds(1, HALF, stride=2), :] = jnp.where(side, swap(left), right)
    return page[...]


def pack(x):
    return jnp.concatenate([x[:HALF], x[HALF:]], axis=1)


def unpack(x):
    return jnp.concatenate([x[:, :RANK], x[:, RANK:]], axis=0)


def visit_order(admissible, leaf, padded_in):
    padded_in[...] = jnp.full(padded_in.shape, -1, jnp.int32)
    padded_in[0:3, 0 : admissible.shape[1]] = admissible[...]
    level = padded_in[0:1, :]
    row = padded_in[1:2, :]
    column = padded_in[2:3, :]
    low = level <= 2
    base = jnp.where(level == 0, 0, jnp.where(level == 1, CL_DEV, CL_DEV + CL_DEV // 2))
    shift = jnp.where(level == 0, 2, jnp.where(level == 1, 1, 0))
    held = jnp.left_shift(1, shift) - 1
    slot = jnp.where(low, base + jnp.bitwise_and(row, held), level + (SLOTS - 3))
    slot = jnp.where(level < 0, -1, slot)
    side = jnp.clip(jnp.right_shift(column, shift) - leaf + 1, 0, 2)
    place = jnp.where(
        low, side * SLOTS + base + jnp.bitwise_and(column, held), 3 * SLOTS + level - 3
    )
    member = lax.broadcasted_iota(jnp.int32, (16, WIDE), 0) == slot
    ahead = lax.broadcasted_iota(jnp.int32, (WIDE, WIDE), 0) <= lax.broadcasted_iota(
        jnp.int32, (WIDE, WIDE), 1
    )
    member_f = jnp.where(member, 1.0, 0.0).astype(F32)
    rank = jnp.dot(member_f.astype(BF16), jnp.where(ahead, 1.0, 0.0).astype(BF16), preferred_element_type=F32)
    count = jnp.sum(member_f, axis=1, keepdims=True)
    even = jnp.floor((count + 1.0) * 0.5) * 2.0
    even = jnp.broadcast_to(even, (16, WIDE)).astype(BF16)
    below = lax.broadcasted_iota(jnp.int32, (16, 16), 1) < lax.broadcasted_iota(jnp.int32, (16, 16), 0)
    begin = jnp.dot(jnp.where(below, 1.0, 0.0).astype(BF16), even, preferred_element_type=F32)
    at = jnp.sum(jnp.where(member, begin + rank - 1.0, 0.0), axis=0, keepdims=True)
    at = jnp.where(slot < 0, -1.0, at).astype(jnp.int32)
    chosen = lax.broadcasted_iota(jnp.int32, (WIDE, WIDE), 0) == at
    line = lax.broadcasted_iota(jnp.int32, (8, WIDE), 0)
    number = lax.broadcasted_iota(jnp.int32, (8, WIDE), 1) + 1
    values = jnp.where(line == 0, number, jnp.where(line == 1, place, jnp.where(line == 2, slot, 0)))
    return lax.dot_general(
        values.astype(F32).astype(BF16), jnp.where(chosen, 1.0, 0.0).astype(BF16),
        (((1,), (1,)), ((), ())), preferred_element_type=F32,
    ).astype(jnp.int32)


def upsweep_kernel(
    leaves, chunk,
    order_in, bottom_in, zero_in, one_in, two_in, three_in,
    grams_to, factors_to,
    order, bottom, zero, one, two, three, grams_out,
    lines, lines_three, page, kids, factors, pairs, tops,
    fetched, stored, send, receive,
):
    me = lax.axis_index("leaf")
    rep = lax.axis_index("rep")
    left = lax.rem(me + leaves - 1, leaves)
    right = lax.rem(me + 1, leaves)
    others = [flipped(me, bits) for bits in range(1, GROUP)]
    start = pl.multiple_of(me // 2 // chunk * chunk, chunk)
    sources = [
        bottom_in, zero_in, order_in, one_in, two_in, three_in.at[pl.ds(start, chunk)],
    ]
    targets = [bottom, zero, order, one, two, three]
    fetches = [
        pltpu.make_async_copy(source, target, fetched.at[k])
        for k, (source, target) in enumerate(zip(sources, targets))
    ]
    for fetch in fetches:
        fetch.start()
    barrier = pltpu.get_barrier_semaphore()
    for other in [left, right] + others:
        pl.semaphore_signal(barrier, inc=1, device_id=(other, rep), device_id_type=MESH)
    for fetch in fetches[:5]:
        fetch.wait()
    tiles_of(bottom, CL_DEV, lines)
    bottoms = [packed(lines, c) for c in range(CL_DEV)]
    leaf_pairs = [natural_pair(bottoms[c], bottoms[c + 1], page) for c in (0, 2)]
    for k in range(2):
        factors[1, k * RANK : (k + 1) * RANK, :] = leaf_pairs[k].astype(BF16)
    tiles_of(zero, CL_DEV, lines)
    zeros = [packed(lines, c) for c in range(CL_DEV)]
    zero_pairs = [natural_pair(zeros[c], zeros[c + 1], page) for c in (0, 2)]
    tiles_of(one, CL_DEV // 2, lines)
    ones = natural_pair(packed(lines, 0), packed(lines, 1), page)
    tiles_of(two, 1, lines)
    own_two = packed(lines, 0)
    twos = natural_pair(own_two, own_two, page)[:, :RANK]

    for c in range(CL_DEV):
        half = slice(c % 2 * RANK, c % 2 * RANK + RANK)
        image = exact_dot(leaf_pairs[c // 2][:, half], zero_pairs[c // 2][:, half])
        kids[c] = exact_gram(image, image)
    level_one = [kids[order[0, 2 * i]] + kids[order[0, 2 * i + 1]] for i in range(2)]
    pairs[1, :RANK, :] = jnp.concatenate(level_one, axis=1)
    level_two = 0.0
    for i in range(2):
        transfer = ones[:, i * RANK : (i + 1) * RANK]
        level_two = level_two + exact_gram(transfer, exact_dot(level_one[i], transfer))
    pairs[1, RANK:, :] = pack(level_two)
    tops[0] = pack(exact_gram(twos, exact_dot(level_two, twos)))

    pl.semaphore_wait(barrier, GROUP + 1)
    copies = []

    def push(source, target, device):
        place = len(copies)
        copy = pltpu.make_async_remote_copy(
            src_ref=source, dst_ref=target, send_sem=send.at[place], recv_sem=receive.at[place],
            device_id=(device, rep), device_id_type=MESH,
        )
        copy.start()
        copies.append(copy)

    for bits in range(1, GROUP):
        push(tops.at[0], tops.at[bits], others[bits - 1])
    push(pairs.at[1], pairs.at[2], left)
    push(pairs.at[1], pairs.at[0], right)
    push(factors.at[1], factors.at[2], left)
    push(factors.at[1], factors.at[0], right)

    fetches[5].wait()
    tiles_of(three, chunk, lines_three)
    place = lax.rem(me // 2, chunk)
    threes = []
    for u in range(GROUP // 2):
        own = packed(lines_three, flipped(place, u))
        threes.append(natural_pair(own, own, page)[:, :RANK])
    for copy in copies[: GROUP - 1]:
        copy.wait_recv()
    level_three, lifted = [], []
    for u in range(GROUP // 2):
        gram = unpack(tops[2 * u] + tops[2 * u + 1])
        level_three.append(gram)
        lifted.append(exact_gram(threes[u], exact_dot(gram, threes[u])))
    level_four = [lifted[0] + lifted[1], lifted[2] + lifted[3]]
    for copy in copies[GROUP - 1 :]:
        copy.wait_recv()
    stores = [pltpu.make_async_copy(factors, factors_to, stored.at[0])]
    stores[0].start()
    for side in range(3):
        grams_out[side * RANK : (side + 1) * RANK, :] = pairs[side, :RANK, :]
    side_two = [unpack(pairs[side, RANK:, :]) for side in range(3)]
    rest = side_two + [level_three[0], level_three[1], level_four[0], level_four[1], level_four[1]]
    for k in range(4):
        at = (3 + k) * RANK
        grams_out[at : at + RANK, :] = jnp.concatenate([rest[2 * k], rest[2 * k + 1]], axis=1)
    grams_out[7 * RANK :, :] = pairs[1, :RANK, :]
    stores.append(pltpu.make_async_copy(grams_out, grams_to, stored.at[1]))
    stores[1].start()
    for store in stores:
        store.wait()
    for copy in copies:
        copy.wait_send()


def upsweep(leaves, order, bottom, zero, one, two, three):
    chunk = min(8, three.shape[0])
    hbm = pl.BlockSpec(memory_space=pltpu.HBM)
    count = GROUP + 3
    return pl.pallas_call(
        functools.partial(upsweep_kernel, leaves, chunk),
        out_shape=[
            jax.ShapeDtypeStruct((8 * RANK, LANES), F32),
            jax.ShapeDtypeStruct((3, LANES, LANES), BF16),
        ],
        in_specs=[hbm] * 6,
        out_specs=[hbm] * 2,
        scratch_shapes=[
            pltpu.SMEM(order.shape, jnp.int32),
            pltpu.VMEM(bottom.shape, F32),
            pltpu.VMEM(zero.shape, F32),
            pltpu.VMEM(one.shape, F32),
            pltpu.VMEM(two.shape, F32),
            pltpu.VMEM((chunk, FLAT), F32),
            pltpu.VMEM((8 * RANK, LANES), F32),
            pltpu.VMEM((HALF * 8, LANES), F32),
            pltpu.VMEM((HALF * 8, LANES), F32),
            pltpu.VMEM((RANK, LANES), F32),
            pltpu.VMEM((CL_DEV, RANK, RANK), F32),
            pltpu.VMEM((3, LANES, LANES), BF16),
            pltpu.VMEM((3, RANK + HALF, LANES), F32),
            pltpu.VMEM((GROUP, HALF, LANES), F32),
            pltpu.SemaphoreType.DMA((6,)),
            pltpu.SemaphoreType.DMA((2,)),
            pltpu.SemaphoreType.DMA((count,)),
            pltpu.SemaphoreType.DMA((count,)),
        ],
        compiler_params=pltpu.CompilerParams(
            collective_id=0, has_side_effects=True, vmem_limit_bytes=60 * MIB
        ),
        name="upsweep",
    )(order, bottom, zero, one, two, three)


def picked(x, index):
    return jnp.take_along_axis(x, index, axis=1, mode="promise_in_bounds")


def factorize(rows):
    lane = lax.broadcasted_iota(jnp.int32, (8, LANES), 1)
    base = jnp.where(lane < RANK, 0, RANK)
    inner = lane - base
    rows = list(rows)
    result = []
    for panel in range(0, RANK, 8):
        entry = {}
        for r in range(8):
            for c in range(r, 8):
                entry[r, c] = picked(rows[panel + r], base + (panel + c))
        done = []
        for k in range(8):
            scale = lax.rsqrt(entry[k, k])
            done.append(rows[panel + k] * scale)
            for c in range(k + 1, 8):
                entry[k, c] = entry[k, c] * scale
            for r in range(k + 1, 8):
                rows[panel + r] = rows[panel + r] - entry[k, r] * done[k]
                for c in range(r, 8):
                    entry[r, c] = entry[r, c] - entry[k, r] * entry[k, c]
        for i in range(panel + 8, RANK):
            for k in range(8):
                rows[i] = rows[i] - picked(done[k], base + i) * done[k]
        for k in range(8):
            result.append(jnp.where(inner >= panel + k, done[k], 0.0))
    return result


def blocks_kernel(
    blocks, pairs,
    admissible_in, grams_in, factors_in, coupling_in,
    projected_to, weights_to,
    admissible, grams, leaf_factors, coupling, projected, weights_out,
    padded_in, visits_v, order, lines, upper, row_table, column_left, column_right,
    own, turned, results, totals, fetched, stored, order_sem,
):
    leaf = lax.axis_index("leaf")
    fetches = [
        pltpu.make_async_copy(source, target, fetched.at[k])
        for k, (source, target) in enumerate((
            (admissible_in, admissible), (grams_in, grams),
            (factors_in, leaf_factors), (coupling_in, coupling),
        ))
    ]
    for fetch in fetches:
        fetch.start()
    side = lanes_left(HALF)
    side_full = lanes_left(RANK)
    lane = lax.broadcasted_iota(jnp.int32, (RANK, LANES), 1)
    inner = jnp.where(lane < RANK, lane, lane - RANK)
    spread = jnp.where(inner < HALF, 2 * inner, 2 * inner - (RANK - 1)) + (lane - inner)

    fetches[0].wait()
    visits_v[...] = visit_order(admissible, leaf, padded_in)
    to_scalar = pltpu.make_async_copy(visits_v, order, order_sem)
    to_scalar.start()
    fetches[1].wait()
    rows = factorize([grams[pl.ds(i, 8, stride=RANK), :] for i in range(RANK)])
    for i in range(RANK):
        upper[i * 8 : (i + 1) * 8, :] = rows[i]

    fetches[3].wait()
    own[0] = jnp.zeros((HALF, LANES), BF16)
    turned[0] = jnp.zeros((HALF, LANES), BF16)

    def lay(group, carry):
        first = pl.multiple_of(group * 16, 16)
        x = coupling[pl.ds(first, 16), :].astype(F32)
        for h in range(2):
            for tile in range(HALF):
                at = (h * HALF + tile) * 8
                lines[at : at + 8, :] = x[8 * h : 8 * h + 8, tile * LANES : (tile + 1) * LANES]
        for s in range(16):
            block = lines[pl.ds(s // 8 * 256 + s % 8, HALF, stride=8), :]
            own[first + s + 1] = block.astype(BF16)
            turned[first + s + 1] = swap(block).astype(BF16)
        return carry

    lax.fori_loop(0, blocks // 16, lay, 0)

    fetches[2].wait()

    def put_column(where, left, right):
        column_left[where] = left.astype(BF16)
        column_right[where] = right.astype(BF16)

    def put_columns(first, second, names):
        flipped_all = jnp.transpose(jnp.concatenate([first, second], axis=0))
        for half in range(2):
            part = flipped_all[half * RANK : (half + 1) * RANK]
            other = swap(part)
            if names[half] is not None:
                put_column(names[half], jnp.where(side_full, part, 0.0), jnp.where(side_full, 0.0, other))
            if names[2 + half] is not None:
                put_column(names[2 + half], jnp.where(side_full, other, 0.0), jnp.where(side_full, 0.0, part))

    def put_rows(even, odd, names):
        x = picked(jnp.concatenate([even, odd], axis=0), spread)
        if names[0] is not None:
            row_table[names[0]] = x.astype(BF16)
        if names[1] is not None:
            row_table[names[1]] = swap(x).astype(BF16)

    for near in range(3):
        first = leaf_factors[near, :RANK, :].astype(F32)
        second = leaf_factors[near, RANK:, :].astype(F32)
        put_columns(first, second, [near * SLOTS + c for c in (0, 1, 2, 3)])
        if near == 1:
            for k, x in enumerate((first, second)):
                lines[k * RANK : (k + 1) * RANK, :] = x
                put_rows(
                    lines[pl.ds(k * RANK, HALF, stride=2), :],
                    lines[pl.ds(k * RANK + 1, HALF, stride=2), :],
                    (2 * k, 2 * k + 1),
                )
    column_names = [
        (4, 5), (SLOTS + 4, SLOTS + 5), (2 * SLOTS + 4, 2 * SLOTS + 5), (6, SLOTS + 6),
        (2 * SLOTS + 6, None), (3 * SLOTS, None), (3 * SLOTS + 1, None), (None, None),
    ]
    for k in range(0, 8, 2):
        put_columns(
            upper[pl.ds(k, RANK, stride=8), :], upper[pl.ds(k + 1, RANK, stride=8), :],
            column_names[k] + column_names[k + 1],
        )
    for k, names in ((1, (4, 5)), (3, (None, 6)), (4, (None, 7)), (5, (None, 8))):
        put_rows(upper[pl.ds(k, HALF, stride=16), :], upper[pl.ds(8 + k, HALF, stride=16), :], names)

    totals[...] = jnp.zeros(totals.shape, F32)
    to_scalar.wait()

    def visits(step, carry):
        places = [step * BATCH + k for k in range(BATCH)]
        halves = []
        for pair in places:
            a, b = order[0, 2 * pair], order[0, 2 * pair + 1]
            both = jnp.concatenate(
                [jnp.where(side, own[a], turned[b]), jnp.where(side, turned[a], own[b])], axis=0
            )
            slot = order[2, 2 * pair]
            halves.append(
                jnp.dot(row_table[slot][:, :RANK], both, preferred_element_type=F32).astype(BF16)
            )
        products = []
        for pair, half in zip(places, halves):
            columns = jnp.concatenate(
                [column_left[order[1, 2 * pair]], column_right[order[1, 2 * pair + 1]]], axis=0
            )
            products.append(jnp.dot(half, columns, preferred_element_type=F32))
        terms = []
        for product in products:
            rounded = product.astype(BF16)
            terms.append(lax.dot_general(
                rounded, rounded, (((1,), (1,)), ((), ())), preferred_element_type=F32
            ))
        for pair, result in zip(places, products):
            a, b = order[0, 2 * pair], order[0, 2 * pair + 1]
            top, bottom = result[:HALF], result[HALF:]
            results[pl.ds(pl.multiple_of(a * HALF, HALF), HALF), :] = jnp.where(side, top, swap(bottom))
            results[pl.ds(pl.multiple_of(b * HALF, HALF), HALF), :] = jnp.where(side, swap(top), bottom)
        for pair, term in zip(places, terms):
            slot = order[2, 2 * pair]
            totals[slot, :, :RANK] += term
        return carry

    lax.fori_loop(0, pairs // BATCH, visits, 0)

    gather = jnp.where(inner % 2 == 0, inner // 2, HALF + inner // 2)
    for s in range(SLOTS):
        x = picked(totals[s], gather)
        weights_out[s * HALF : (s + 1) * HALF, :] = jnp.where(side, x[:HALF], x[HALF:]) * (1.0 / RANK)
    groups = blocks // 16
    weights_store = pltpu.make_async_copy(weights_out, weights_to, stored.at[groups])
    weights_store.start()

    def store_of(group):
        span = pl.ds(pl.multiple_of(group * 16, 16), 16)
        return pltpu.make_async_copy(projected.at[span], projected_to.at[span], stored.at[group])

    def write(group, carry):
        first = pl.multiple_of(group * 16, 16)
        for tile in range(HALF):
            at = (first + 1) * HALF + tile
            x = jnp.concatenate(
                [
                    results[pl.ds(at, 8, stride=HALF), :],
                    results[pl.ds(at + 8 * HALF, 8, stride=HALF), :],
                ],
                axis=0,
            )
            projected[pl.ds(first, 16), tile * LANES : (tile + 1) * LANES] = x.astype(BF16)
        store_of(group).start()
        return carry

    lax.fori_loop(0, groups, write, 0)
    weights_store.wait()
    for group in range(groups):
        store_of(group).wait()


def blocks_call(admissible, grams, leaf_factors, coupling):
    blocks = coupling.shape[0]
    pairs = -(-(blocks + ROW_SLOTS) // 2)
    pairs = -(-pairs // BATCH) * BATCH
    hbm = pl.BlockSpec(memory_space=pltpu.HBM)
    return pl.pallas_call(
        functools.partial(blocks_kernel, blocks, pairs),
        out_shape=[
            jax.ShapeDtypeStruct((blocks, FLAT), BF16),
            jax.ShapeDtypeStruct((SLOTS * HALF, LANES), F32),
        ],
        in_specs=[hbm] * 4,
        out_specs=[hbm] * 2,
        scratch_shapes=[
            pltpu.VMEM(admissible.shape, jnp.int32),
            pltpu.VMEM(grams.shape, F32),
            pltpu.VMEM(leaf_factors.shape, BF16),
            pltpu.VMEM(coupling.shape, BF16),
            pltpu.VMEM(coupling.shape, BF16),
            pltpu.VMEM((SLOTS * HALF, LANES), F32),
            pltpu.VMEM((8, WIDE), jnp.int32),
            pltpu.VMEM((8, WIDE), jnp.int32),
            pltpu.SMEM((8, WIDE), jnp.int32),
            pltpu.VMEM((512, LANES), F32),
            pltpu.VMEM((512, LANES), F32),
            pltpu.VMEM((ROW_SLOTS, RANK, LANES), BF16),
            pltpu.VMEM((COLUMNS, RANK, LANES), BF16),
            pltpu.VMEM((COLUMNS, RANK, LANES), BF16),
            pltpu.VMEM((blocks + 1, HALF, LANES), BF16),
            pltpu.VMEM((blocks + 1, HALF, LANES), BF16),
            pltpu.VMEM(((blocks + 1) * HALF, LANES), F32),
            pltpu.VMEM((ROW_SLOTS, RANK, LANES), F32),
            pltpu.SemaphoreType.DMA((4,)),
            pltpu.SemaphoreType.DMA((blocks // 16 + 1,)),
            pltpu.SemaphoreType.DMA,
        ],
        compiler_params=pltpu.CompilerParams(vmem_limit_bytes=60 * MIB),
        name="blocks",
    )(admissible, grams, leaf_factors, coupling)


def sum_kernel(reps, part, total, parts, send, receive):
    leaf = lax.axis_index("leaf")
    me = lax.axis_index("rep")
    barrier = pltpu.get_barrier_semaphore()
    for step in range(1, reps):
        other = lax.rem(me + step, reps)
        pl.semaphore_signal(barrier, inc=1, device_id=(leaf, other), device_id_type=MESH)
    parts[me] = part[...].astype(BF16)
    pl.semaphore_wait(barrier, reps - 1)
    copies = []
    for step in range(1, reps):
        copy = pltpu.make_async_remote_copy(
            src_ref=parts.at[me], dst_ref=parts.at[me],
            send_sem=send.at[step - 1], recv_sem=receive.at[step - 1],
            device_id=(leaf, lax.rem(me + step, reps)), device_id_type=MESH,
        )
        copy.start()
        copies.append(copy)
    for copy in copies:
        copy.wait_recv()
    added = parts[0].astype(F32)
    for k in range(1, reps):
        added = added + parts[k].astype(F32)
    total[...] = added
    for copy in copies:
        copy.wait_send()


def sum_call(reps, part):
    return pl.pallas_call(
        functools.partial(sum_kernel, reps),
        out_shape=jax.ShapeDtypeStruct(part.shape, F32),
        in_specs=[pl.BlockSpec(memory_space=pltpu.VMEM)],
        out_specs=pl.BlockSpec(memory_space=pltpu.VMEM),
        scratch_shapes=[
            pltpu.VMEM((reps,) + part.shape, BF16),
            pltpu.SemaphoreType.DMA((reps - 1,)),
            pltpu.SemaphoreType.DMA((reps - 1,)),
        ],
        compiler_params=pltpu.CompilerParams(
            collective_id=1, has_side_effects=True, vmem_limit_bytes=16 * MIB
        ),
        name="rep_sum",
    )(part)


def deliver_kernel(total, zero, one, two, zero_v, one_v, two_v, sems):
    for tile in range(HALF):
        span = slice(tile * LANES, (tile + 1) * LANES)
        zero_v[:, span] = total[pl.ds(tile, CL_DEV, stride=HALF), :]
        one_v[:, span] = total[pl.ds(tile + CL_DEV * HALF, CL_DEV // 2, stride=HALF), :]
        at = tile + (SLOTS - 1) * HALF
        two_v[:, span] = total[at : at + 1, :]
    copies = [
        pltpu.make_async_copy(source, target, sems.at[k])
        for k, (source, target) in enumerate(((zero_v, zero), (one_v, one), (two_v, two)))
    ]
    for copy in copies:
        copy.start()
    for copy in copies:
        copy.wait()


def deliver_call(total):
    small = [(count, FLAT) for count in (CL_DEV, CL_DEV // 2, 1)]
    return pl.pallas_call(
        deliver_kernel,
        out_shape=[jax.ShapeDtypeStruct(shape, F32) for shape in small],
        in_specs=[pl.BlockSpec(memory_space=pltpu.VMEM)],
        out_specs=[pl.BlockSpec(memory_space=pltpu.HBM)] * 3,
        scratch_shapes=[pltpu.VMEM(shape, F32) for shape in small] + [pltpu.SemaphoreType.DMA((3,))],
        name="deliver",
    )(total)


def local(leaves, reps, bottom, zero, one, two, three, order, coupling, admissible):
    grams, leaf_factors = upsweep(leaves, order, bottom, zero, one, two, three)
    projected, part = blocks_call(admissible, grams, leaf_factors, coupling)
    return projected, *deliver_call(sum_call(reps, part))


def solution(mesh):
    return jax.shard_map(
        functools.partial(local, mesh.shape["leaf"], mesh.shape["rep"]),
        mesh=mesh,
        in_specs=(
            P("leaf", None),
            P("leaf", None),
            P("leaf", None),
            P("leaf", None),
            P(),
            P("leaf", None),
            P(("leaf", "rep"), None),
            P(None, ("leaf", "rep")),
        ),
        out_specs=(P(("leaf", "rep"), None), P("leaf", None), P("leaf", None), P("leaf", None)),
        check_vma=False,
    )
```

```python
import functools

import jax
import jax.numpy as jnp
from jax import lax
from jax.experimental import pallas as pl
from jax.experimental.pallas import tpu as pltpu
from jax.sharding import PartitionSpec as P

RANK = 64
HALF = 32
LANES = 128
FLAT = RANK * RANK
CL_DEV = 4
SLOTS = 7
ROW_SLOTS = 9
COLUMNS = 3 * SLOTS + 2
GROUP = 8
MESH = pl.DeviceIdType.MESH
F32 = jnp.float32
BF16 = jnp.bfloat16
EXACT = lax.Precision.HIGHEST
WIDE = 256
BATCH = 25
MIB = 1024 * 1024


def lanes_left(rows):
    return lax.broadcasted_iota(jnp.int32, (rows, LANES), 1) < RANK


def swap(x):
    return pltpu.roll(x, RANK, 1)


def exact_dot(a, b):
    return jnp.dot(a, b, precision=EXACT, preferred_element_type=F32)


def exact_gram(a, b):
    return lax.dot_general(a, b, (((0,), (0,)), ((), ())), precision=EXACT, preferred_element_type=F32)


def flipped(index, bits):
    result = index
    for place in range(3):
        if bits >> place & 1:
            result = result + (1 - 2 * (index // (1 << place) % 2)) * (1 << place)
    return result


def tiles_of(flat, rows, lines):
    for tile in range(HALF):
        lines[tile * 8 : tile * 8 + rows, :] = flat[:, tile * LANES : (tile + 1) * LANES]


def packed(lines, which):
    return lines[pl.ds(which, HALF, stride=8), :]


def natural_pair(left, right, page):
    side = lanes_left(HALF)
    page[pl.ds(0, HALF, stride=2), :] = jnp.where(side, left, swap(right))
    page[pl.ds(1, HALF, stride=2), :] = jnp.where(side, swap(left), right)
    return page[...]


def pack(x):
    return jnp.concatenate([x[:HALF], x[HALF:]], axis=1)


def unpack(x):
    return jnp.concatenate([x[:, :RANK], x[:, RANK:]], axis=0)


def picked(x, index):
    return jnp.take_along_axis(x, index, axis=1, mode="promise_in_bounds")


def factorize(rows, upper):
    lane = lax.broadcasted_iota(jnp.int32, (8, LANES), 1)
    base = jnp.where(lane < RANK, 0, RANK)
    inner = lane - base
    all_rows = RANK * 8
    tall_base = jnp.where(lax.broadcasted_iota(jnp.int32, (all_rows, LANES), 1) < RANK, 0, RANK)
    tall_index = tall_base + lax.broadcasted_iota(jnp.int32, (all_rows, LANES), 0) // 8
    rest = jnp.concatenate(rows, axis=0)
    for panel in range(0, RANK, 8):
        block = [rest[r * 8 : (r + 1) * 8] for r in range(8)]
        rest = rest[RANK:] if panel + 8 < RANK else None
        entry = {}
        for r in range(8):
            for c in range(r, 8):
                entry[r, c] = picked(block[r], base + (panel + c))
        done = []
        for k in range(8):
            scale = lax.rsqrt(entry[k, k])
            done.append(block[k] * scale)
            for c in range(k + 1, 8):
                entry[k, c] = entry[k, c] * scale
            for r in range(k + 1, 8):
                block[r] = block[r] - entry[k, r] * done[k]
                for c in range(r, 8):
                    entry[r, c] = entry[r, c] - entry[k, r] * entry[k, c]
        if rest is not None:
            index = tall_index[RANK + panel * 8 :]
            for k in range(8):
                tall = jnp.concatenate([done[k]] * (RANK - panel - 8), axis=0)
                rest = rest - picked(tall, index) * tall
        for k in range(8):
            at = (panel + k) * 8
            upper[at : at + 8, :] = jnp.where(inner >= panel + k, done[k], 0.0)


def visit_order(admissible, leaf, padded_in, blocks, empty):
    padded_in[...] = jnp.full(padded_in.shape, -1, jnp.int32)
    padded_in[0:3, 0 : admissible.shape[1]] = admissible[...]
    level = padded_in[0:1, :]
    row = padded_in[1:2, :]
    column = padded_in[2:3, :]
    low = level <= 2
    base = jnp.where(level == 0, 0, jnp.where(level == 1, CL_DEV, CL_DEV + CL_DEV // 2))
    shift = jnp.where(level == 0, 2, jnp.where(level == 1, 1, 0))
    held = jnp.left_shift(1, shift) - 1
    slot = jnp.where(low, base + jnp.bitwise_and(row, held), level + (SLOTS - 3))
    slot = jnp.where(level < 0, -1, slot)
    side = jnp.minimum(jnp.maximum(jnp.right_shift(column, shift) - leaf + 1, 0), 2)
    place = jnp.where(
        low, side * SLOTS + base + jnp.bitwise_and(column, held), 3 * SLOTS + level - 3
    )
    member = lax.broadcasted_iota(jnp.int32, (16, WIDE), 0) == slot
    ahead = lax.broadcasted_iota(jnp.int32, (WIDE, WIDE), 0) <= lax.broadcasted_iota(
        jnp.int32, (WIDE, WIDE), 1
    )
    member_f = jnp.where(member, 1.0, 0.0).astype(F32)
    rank = jnp.dot(member_f.astype(BF16), jnp.where(ahead, 1.0, 0.0).astype(BF16), preferred_element_type=F32)
    count = jnp.sum(member_f, axis=1, keepdims=True)
    even = jnp.floor((count + 1.0) * 0.5) * 2.0
    even = jnp.broadcast_to(even, (16, WIDE)).astype(BF16)
    below = lax.broadcasted_iota(jnp.int32, (16, 16), 1) < lax.broadcasted_iota(jnp.int32, (16, 16), 0)
    begin = jnp.dot(jnp.where(below, 1.0, 0.0).astype(BF16), even, preferred_element_type=F32)
    at = jnp.sum(jnp.where(member, begin + rank - 1.0, 0.0), axis=0, keepdims=True)
    at = jnp.where(slot < 0, -1.0, at).astype(jnp.int32)
    chosen = lax.broadcasted_iota(jnp.int32, (WIDE, WIDE), 0) == at
    line = lax.broadcasted_iota(jnp.int32, (8, WIDE), 0)
    lane = lax.broadcasted_iota(jnp.int32, (8, WIDE), 1)
    values = jnp.where(line == 0, lane + 1, jnp.where(line == 1, place, jnp.where(line == 2, slot, 0)))
    listed = lax.dot_general(
        values.astype(F32).astype(BF16), jnp.where(chosen, 1.0, 0.0).astype(BF16),
        (((1,), (1,)), ((), ())), preferred_element_type=F32,
    )
    same = jnp.where(listed[2:3] == pltpu.roll(listed, 2, 1)[2:3], 1.0, 0.0)
    last = jnp.where(count > 0.0, (begin + even.astype(F32)) * 0.5 - 1.0, float(empty))
    diagonal = lax.broadcasted_iota(jnp.int32, (16, WIDE), 0) == lax.broadcasted_iota(
        jnp.int32, (16, WIDE), 1
    )
    last = jnp.sum(jnp.where(diagonal, last, 0.0), axis=0, keepdims=True)
    listed = jnp.where(line == 3, same, jnp.where(line == 4, last, listed))
    listed = jnp.where(line == 5, at, listed.astype(jnp.int32))
    limits = (blocks, COLUMNS - 1, ROW_SLOTS - 1, 1, empty, 2 * empty - 1)
    limit = jnp.zeros(line.shape, jnp.int32)
    for k, most in enumerate(limits):
        limit = jnp.where(line == k, most, limit)
    return jnp.minimum(jnp.maximum(listed, 0), limit)


def main_kernel(
    leaves, reps, blocks, chunk, pairs,
    order_in, bottom_in, zero_in, one_in, two_in, three_in, admissible_in, coupling_in,
    projected_to, weights_zero, weights_one, weights_two,
    child, bottom, zero, one, two, three, admissible, coupling, projected, zero_v, one_v, two_v,
    lines, lines_three, page, kids, factors, near, tops, grams, upper,
    padded_in, visits_v, order, row_table, column_left, column_right,
    own, turned, results, snapshots, parts, total,
    fetched, stored, order_sem, send, receive, share_send, share_receive,
):
    me = lax.axis_index("leaf")
    rep = lax.axis_index("rep")
    left = lax.rem(me + leaves - 1, leaves)
    right = lax.rem(me + 1, leaves)
    others = [flipped(me, bits) for bits in range(1, GROUP)]
    start = pl.multiple_of(me // 2 // chunk * chunk, chunk)
    fetches = [
        pltpu.make_async_copy(source, target, fetched.at[k])
        for k, (source, target) in enumerate((
            (bottom_in, bottom), (zero_in, zero), (order_in, child), (one_in, one), (two_in, two),
            (three_in.at[pl.ds(start, chunk)], three), (admissible_in, admissible),
            (coupling_in, coupling),
        ))
    ]
    for fetch in fetches:
        fetch.start()
    barrier = pltpu.get_barrier_semaphore()
    for other in [left, right] + others:
        pl.semaphore_signal(barrier, inc=1, device_id=(other, rep), device_id_type=MESH)
    for step in range(1, reps):
        other = lax.rem(rep + step, reps)
        pl.semaphore_signal(barrier, inc=1, device_id=(me, other), device_id_type=MESH)
    for fetch in fetches[:5]:
        fetch.wait()

    tiles_of(bottom, CL_DEV, lines)
    bottoms = [packed(lines, c) for c in range(CL_DEV)]
    leaf_pairs = [natural_pair(bottoms[c], bottoms[c + 1], page) for c in (0, 2)]
    for k in range(2):
        factors[1, k * RANK : (k + 1) * RANK, :] = leaf_pairs[k].astype(BF16)
    tiles_of(zero, CL_DEV, lines)
    zeros = [packed(lines, c) for c in range(CL_DEV)]
    zero_pairs = [natural_pair(zeros[c], zeros[c + 1], page) for c in (0, 2)]
    tiles_of(one, CL_DEV // 2, lines)
    ones = natural_pair(packed(lines, 0), packed(lines, 1), page)
    tiles_of(two, 1, lines)
    own_two = packed(lines, 0)
    twos = natural_pair(own_two, own_two, page)[:, :RANK]

    for c in range(CL_DEV):
        half = slice(c % 2 * RANK, c % 2 * RANK + RANK)
        image = exact_dot(leaf_pairs[c // 2][:, half], zero_pairs[c // 2][:, half])
        kids[c] = exact_gram(image, image)
    level_one = [kids[child[0, 2 * i]] + kids[child[0, 2 * i + 1]] for i in range(2)]
    near[1, :RANK, :] = jnp.concatenate(level_one, axis=1)
    level_two = 0.0
    for i in range(2):
        transfer = ones[:, i * RANK : (i + 1) * RANK]
        level_two = level_two + exact_gram(transfer, exact_dot(level_one[i], transfer))
    near[1, RANK:, :] = pack(level_two)
    tops[0] = pack(exact_gram(twos, exact_dot(level_two, twos)))

    pl.semaphore_wait(barrier, GROUP + reps)
    copies = []

    def push(source, target, device):
        place = len(copies)
        copy = pltpu.make_async_remote_copy(
            src_ref=source, dst_ref=target, send_sem=send.at[place], recv_sem=receive.at[place],
            device_id=(device, rep), device_id_type=MESH,
        )
        copy.start()
        copies.append(copy)

    for bits in range(1, GROUP):
        push(tops.at[0], tops.at[bits], others[bits - 1])
    push(near.at[1], near.at[2], left)
    push(near.at[1], near.at[0], right)
    push(factors.at[1], factors.at[2], left)
    push(factors.at[1], factors.at[0], right)

    fetches[6].wait()
    visits_v[...] = visit_order(admissible, me, padded_in, blocks, pairs)
    to_scalar = pltpu.make_async_copy(visits_v, order, order_sem)
    to_scalar.start()
    fetches[7].wait()
    own[0] = jnp.zeros((HALF, LANES), BF16)
    turned[0] = jnp.zeros((HALF, LANES), BF16)

    def lay(group, carry):
        first = pl.multiple_of(group * 16, 16)
        x = coupling[pl.ds(first, 16), :].astype(F32)
        for h in range(2):
            for tile in range(HALF):
                at = (h * HALF + tile) * 8
                lines[at : at + 8, :] = x[8 * h : 8 * h + 8, tile * LANES : (tile + 1) * LANES]
        for s in range(16):
            block = lines[pl.ds(s // 8 * 256 + s % 8, HALF, stride=8), :]
            own[first + s + 1] = block.astype(BF16)
            turned[first + s + 1] = swap(block).astype(BF16)
        return carry

    lax.fori_loop(0, blocks // 16, lay, 0)

    fetches[5].wait()
    tiles_of(three, chunk, lines_three)
    place = lax.rem(me // 2, chunk)
    threes = []
    for u in range(GROUP // 2):
        matrix = packed(lines_three, flipped(place, u))
        threes.append(natural_pair(matrix, matrix, page)[:, :RANK])
    for copy in copies[: GROUP - 1]:
        copy.wait_recv()
    level_three, lifted = [], []
    for u in range(GROUP // 2):
        gram = unpack(tops[2 * u] + tops[2 * u + 1])
        level_three.append(gram)
        lifted.append(exact_gram(threes[u], exact_dot(gram, threes[u])))
    level_four = [lifted[0] + lifted[1], lifted[2] + lifted[3]]
    for copy in copies[GROUP - 1 :]:
        copy.wait_recv()
    for side in range(3):
        grams[side * RANK : (side + 1) * RANK, :] = near[side, :RANK, :]
    side_two = [unpack(near[side, RANK:, :]) for side in range(3)]
    rest = side_two + [level_three[0], level_three[1], level_four[0], level_four[1], level_four[1]]
    for k in range(4):
        at = (3 + k) * RANK
        grams[at : at + RANK, :] = jnp.concatenate([rest[2 * k], rest[2 * k + 1]], axis=1)
    grams[7 * RANK :, :] = near[1, :RANK, :]

    side = lanes_left(HALF)
    side_full = lanes_left(RANK)
    lane = lax.broadcasted_iota(jnp.int32, (RANK, LANES), 1)
    inner = jnp.where(lane < RANK, lane, lane - RANK)
    spread = jnp.where(inner < HALF, 2 * inner, 2 * inner - (RANK - 1)) + (lane - inner)

    factorize([grams[pl.ds(i, 8, stride=RANK), :] for i in range(RANK)], upper)

    def put_column(where, left, right):
        column_left[where] = left.astype(BF16)
        column_right[where] = right.astype(BF16)

    def put_columns(first, second, names):
        flipped_all = jnp.transpose(jnp.concatenate([first, second], axis=0))
        for half in range(2):
            part = flipped_all[half * RANK : (half + 1) * RANK]
            other = swap(part)
            if names[half] is not None:
                put_column(names[half], jnp.where(side_full, part, 0.0), jnp.where(side_full, 0.0, other))
            if names[2 + half] is not None:
                put_column(names[2 + half], jnp.where(side_full, other, 0.0), jnp.where(side_full, 0.0, part))

    def put_rows(even, odd, names):
        x = picked(jnp.concatenate([even, odd], axis=0), spread)
        if names[0] is not None:
            row_table[names[0]] = x.astype(BF16)
        if names[1] is not None:
            row_table[names[1]] = swap(x).astype(BF16)

    for near_by in range(3):
        first = factors[near_by, :RANK, :].astype(F32)
        second = factors[near_by, RANK:, :].astype(F32)
        put_columns(first, second, [near_by * SLOTS + c for c in (0, 1, 2, 3)])
        if near_by == 1:
            for k, x in enumerate((first, second)):
                lines[k * RANK : (k + 1) * RANK, :] = x
                put_rows(
                    lines[pl.ds(k * RANK, HALF, stride=2), :],
                    lines[pl.ds(k * RANK + 1, HALF, stride=2), :],
                    (2 * k, 2 * k + 1),
                )
    column_names = [
        (4, 5), (SLOTS + 4, SLOTS + 5), (2 * SLOTS + 4, 2 * SLOTS + 5), (6, SLOTS + 6),
        (2 * SLOTS + 6, None), (3 * SLOTS, None), (3 * SLOTS + 1, None), (None, None),
    ]
    for k in range(0, 8, 2):
        put_columns(
            upper[pl.ds(k, RANK, stride=8), :], upper[pl.ds(k + 1, RANK, stride=8), :],
            column_names[k] + column_names[k + 1],
        )
    for k, names in ((1, (4, 5)), (3, (None, 6)), (4, (None, 7)), (5, (None, 8))):
        put_rows(upper[pl.ds(k, HALF, stride=16), :], upper[pl.ds(8 + k, HALF, stride=16), :], names)

    snapshots[pairs] = jnp.zeros((RANK, LANES), F32)
    to_scalar.wait()

    def visits(step, carry):
        places = [step * BATCH + k for k in range(BATCH)]
        halves = []
        for pair in places:
            a, b = order[0, 2 * pair], order[0, 2 * pair + 1]
            both = jnp.concatenate(
                [jnp.where(side, own[a], turned[b]), jnp.where(side, turned[a], own[b])], axis=0
            )
            slot = order[2, 2 * pair]
            halves.append(
                jnp.dot(row_table[slot][:, :RANK], both, preferred_element_type=F32).astype(BF16)
            )
        products = []
        for pair, half in zip(places, halves):
            columns = jnp.concatenate(
                [column_left[order[1, 2 * pair]], column_right[order[1, 2 * pair + 1]]], axis=0
            )
            products.append(jnp.dot(half, columns, preferred_element_type=F32))
        terms = []
        for product in products:
            rounded = product.astype(BF16)
            terms.append(lax.dot_general(
                rounded, rounded, (((1,), (1,)), ((), ())), preferred_element_type=F32
            ))
        for pair, result in zip(places, products):
            top, bottom_half = result[:HALF], result[HALF:]
            results[2 * pair] = jnp.where(side, top, swap(bottom_half))
            results[2 * pair + 1] = jnp.where(side, swap(top), bottom_half)
        for pair, term in zip(places, terms):
            carry = carry * order[3, 2 * pair].astype(F32) + term
            snapshots[pair, :, :RANK] = carry
        return carry

    lax.fori_loop(0, pairs // BATCH, visits, jnp.zeros((RANK, RANK), F32))

    gather = jnp.where(inner % 2 == 0, inner // 2, HALF + inner // 2)
    for s in range(SLOTS):
        x = picked(snapshots[order[4, s]], gather)
        part = jnp.where(side, x[:HALF], x[HALF:]) * (1.0 / RANK)
        parts[rep, s * HALF : (s + 1) * HALF, :] = part.astype(BF16)
    shares = []
    for step in range(1, reps):
        copy = pltpu.make_async_remote_copy(
            src_ref=parts.at[rep], dst_ref=parts.at[rep],
            send_sem=share_send.at[step - 1], recv_sem=share_receive.at[step - 1],
            device_id=(me, lax.rem(rep + step, reps)), device_id_type=MESH,
        )
        copy.start()
        shares.append(copy)

    def store_of(group):
        span = pl.ds(pl.multiple_of(group * 16, 16), 16)
        return pltpu.make_async_copy(projected.at[span], projected_to.at[span], stored.at[group])

    def write(group, carry):
        first = pl.multiple_of(group * 16, 16)
        for s in range(16):
            lines[s * HALF : (s + 1) * HALF, :] = results[order[5, first + s]]
        for tile in range(HALF):
            x = jnp.concatenate(
                [
                    lines[pl.ds(tile, 8, stride=HALF), :],
                    lines[pl.ds(tile + 8 * HALF, 8, stride=HALF), :],
                ],
                axis=0,
            )
            projected[pl.ds(first, 16), tile * LANES : (tile + 1) * LANES] = x.astype(BF16)
        store_of(group).start()
        return carry

    groups = blocks // 16
    lax.fori_loop(0, groups, write, 0)
    for copy in shares:
        copy.wait_recv()
    added = parts[0].astype(F32)
    for k in range(1, reps):
        added = added + parts[k].astype(F32)
    total[...] = added
    for tile in range(HALF):
        span = slice(tile * LANES, (tile + 1) * LANES)
        zero_v[:, span] = total[pl.ds(tile, CL_DEV, stride=HALF), :]
        one_v[:, span] = total[pl.ds(tile + CL_DEV * HALF, CL_DEV // 2, stride=HALF), :]
        at = tile + (SLOTS - 1) * HALF
        two_v[:, span] = total[at : at + 1, :]
    stores = [
        pltpu.make_async_copy(source, target, stored.at[groups + k])
        for k, (source, target) in enumerate(
            ((zero_v, weights_zero), (one_v, weights_one), (two_v, weights_two))
        )
    ]
    for store in stores:
        store.start()
    for copy in copies + shares:
        copy.wait_send()
    for store in stores + [store_of(group) for group in range(groups)]:
        store.wait()


def main_call(leaves, reps, order, bottom, zero, one, two, three, admissible, coupling):
    chunk = min(8, three.shape[0])
    blocks = coupling.shape[0]
    pairs = (blocks + ROW_SLOTS) // 2
    pairs = -(-pairs // BATCH) * BATCH
    hbm = pl.BlockSpec(memory_space=pltpu.HBM)
    small = [jax.ShapeDtypeStruct((count, FLAT), F32) for count in (CL_DEV, CL_DEV // 2, 1)]
    count = GROUP + 3
    whole = [bottom, zero, one, two]
    return pl.pallas_call(
        functools.partial(main_kernel, leaves, reps, blocks, chunk, pairs),
        out_shape=[jax.ShapeDtypeStruct((blocks, FLAT), BF16)] + small,
        in_specs=[hbm] * 8,
        out_specs=[hbm] * 4,
        scratch_shapes=[
            pltpu.SMEM(order.shape, jnp.int32),
            *[pltpu.VMEM(x.shape, x.dtype) for x in whole],
            pltpu.VMEM((chunk, FLAT), F32),
            pltpu.VMEM(admissible.shape, jnp.int32),
            pltpu.VMEM(coupling.shape, BF16),
            pltpu.VMEM(coupling.shape, BF16),
            *[pltpu.VMEM(x.shape, F32) for x in small],
            pltpu.VMEM((512, LANES), F32),
            pltpu.VMEM((HALF * 8, LANES), F32),
            pltpu.VMEM((RANK, LANES), F32),
            pltpu.VMEM((CL_DEV, RANK, RANK), F32),
            pltpu.VMEM((3, LANES, LANES), BF16),
            pltpu.VMEM((3, RANK + HALF, LANES), F32),
            pltpu.VMEM((GROUP, HALF, LANES), F32),
            pltpu.VMEM((8 * RANK, LANES), F32),
            pltpu.VMEM((8 * RANK, LANES), F32),
            pltpu.VMEM((8, WIDE), jnp.int32),
            pltpu.VMEM((8, WIDE), jnp.int32),
            pltpu.SMEM((8, WIDE), jnp.int32),
            pltpu.VMEM((ROW_SLOTS, RANK, LANES), BF16),
            pltpu.VMEM((COLUMNS, RANK, LANES), BF16),
            pltpu.VMEM((COLUMNS, RANK, LANES), BF16),
            pltpu.VMEM((blocks + 1, HALF, LANES), BF16),
            pltpu.VMEM((blocks + 1, HALF, LANES), BF16),
            pltpu.VMEM((2 * pairs, HALF, LANES), F32),
            pltpu.VMEM((pairs + 1, RANK, LANES), F32),
            pltpu.VMEM((reps, SLOTS * HALF, LANES), BF16),
            pltpu.VMEM((SLOTS * HALF, LANES), F32),
            pltpu.SemaphoreType.DMA((8,)),
            pltpu.SemaphoreType.DMA((blocks // 16 + 3,)),
            pltpu.SemaphoreType.DMA,
            pltpu.SemaphoreType.DMA((count,)),
            pltpu.SemaphoreType.DMA((count,)),
            pltpu.SemaphoreType.DMA((reps - 1,)),
            pltpu.SemaphoreType.DMA((reps - 1,)),
        ],
        compiler_params=pltpu.CompilerParams(
            collective_id=0, has_side_effects=True, vmem_limit_bytes=60 * MIB
        ),
        name="upsweep_and_blocks",
    )(order, bottom, zero, one, two, three, admissible, coupling)


def deliver_kernel(parts, *refs):
    count = len(refs) // 3
    sources, targets, held = refs[:count], refs[count : 2 * count], refs[2 * count : 3 * count]
    came, went = refs[3 * count :]
    rows = sources[0].shape[0] // parts
    spans = [(0, pl.ds(k * rows, rows)) for k in range(parts)]
    spans += [(k, pl.ds(0, sources[k].shape[0])) for k in range(1, count)]
    reads = [
        pltpu.make_async_copy(sources[k].at[span], held[k].at[span], came.at[n])
        for n, (k, span) in enumerate(spans)
    ]
    writes = [
        pltpu.make_async_copy(held[k].at[span], targets[k].at[span], went.at[n])
        for n, (k, span) in enumerate(spans)
    ]
    for read in reads:
        read.start()
    for read, write in zip(reads, writes):
        read.wait()
        write.start()
    for write in writes:
        write.wait()


def deliver_call(*arrays):
    hbm = pl.BlockSpec(memory_space=pltpu.HBM)
    parts = 4
    moves = len(arrays) - 1 + parts
    return pl.pallas_call(
        functools.partial(deliver_kernel, parts),
        out_shape=[jax.ShapeDtypeStruct(x.shape, x.dtype) for x in arrays],
        in_specs=[hbm] * len(arrays),
        out_specs=[hbm] * len(arrays),
        scratch_shapes=[pltpu.VMEM(x.shape, x.dtype) for x in arrays]
        + [pltpu.SemaphoreType.DMA((moves,))] * 2,
        compiler_params=pltpu.CompilerParams(vmem_limit_bytes=60 * MIB),
        name="deliver",
    )(*arrays)


def local(leaves, reps, bottom, zero, one, two, three, order, coupling, admissible):
    return tuple(deliver_call(
        *main_call(leaves, reps, order, bottom, zero, one, two, three, admissible, coupling)
    ))


def solution(mesh):
    return jax.shard_map(
        functools.partial(local, mesh.shape["leaf"], mesh.shape["rep"]),
        mesh=mesh,
        in_specs=(
            P("leaf", None),
            P("leaf", None),
            P("leaf", None),
            P("leaf", None),
            P(),
            P("leaf", None),
            P(("leaf", "rep"), None),
            P(None, ("leaf", "rep")),
        ),
        out_specs=(P(("leaf", "rep"), None), P("leaf", None), P("leaf", None), P("leaf", None)),
        check_vma=False,
    )
```

```python
import functools

import jax
import jax.numpy as jnp
from jax import lax
from jax.experimental import pallas as pl
from jax.experimental.pallas import tpu as pltpu
from jax.sharding import PartitionSpec as P

RANK = 64
HALF = 32
LANES = 128
FLAT = RANK * RANK
CL_DEV = 4
SLOTS = 7
ROW_SLOTS = 9
COLUMNS = 3 * SLOTS + 2
GROUP = 8
MESH = pl.DeviceIdType.MESH
F32 = jnp.float32
BF16 = jnp.bfloat16
EXACT = lax.Precision.HIGHEST
WIDE = 256
BATCH = 100
PITCH = 72
APART = 40
MIB = 1024 * 1024


def lanes_left(rows):
    return lax.broadcasted_iota(jnp.int32, (rows, LANES), 1) < RANK


def swap(x):
    return pltpu.roll(x, RANK, 1)


def exact_dot(a, b):
    return jnp.dot(a, b, precision=EXACT, preferred_element_type=F32)


def exact_gram(a, b):
    return lax.dot_general(a, b, (((0,), (0,)), ((), ())), precision=EXACT, preferred_element_type=F32)


def flipped(index, bits):
    result = index
    for place in range(3):
        if bits >> place & 1:
            result = result + (1 - 2 * (index // (1 << place) % 2)) * (1 << place)
    return result


def tiles_of(flat, rows, lines):
    for tile in range(HALF):
        lines[tile * 8 : tile * 8 + rows, :] = flat[:, tile * LANES : (tile + 1) * LANES]


def packed(lines, which):
    return lines[pl.ds(which, HALF, stride=8), :]


def natural_pair(left, right, page):
    side = lanes_left(HALF)
    page[pl.ds(0, HALF, stride=2), :] = jnp.where(side, left, swap(right))
    page[pl.ds(1, HALF, stride=2), :] = jnp.where(side, swap(left), right)
    return page[...]


def pack(x):
    return jnp.concatenate([x[:HALF], x[HALF:]], axis=1)


def unpack(x):
    return jnp.concatenate([x[:, :RANK], x[:, RANK:]], axis=0)


def picked(x, index):
    return jnp.take_along_axis(x, index, axis=1, mode="promise_in_bounds")


def added(terms):
    while len(terms) > 1:
        terms = [sum(terms[k + 1 : k + 2], terms[k]) for k in range(0, len(terms), 2)]
    return terms[0]


def factorize_rows(rows, first, last, upper):
    lane = lax.broadcasted_iota(jnp.int32, (8, LANES), 1)
    base = jnp.where(lane < RANK, 0, RANK)
    inner = lane - base
    pivots = [(r, c) for r in range(8) for c in range(r, 8)]
    entry = {(r, c): picked(rows[first + r], base + (first + c)) for r, c in pivots}
    for panel in range(first, last, 8):
        block = rows[panel : panel + 8]
        done = []
        for k in range(8):
            scale = lax.rsqrt(entry[k, k])
            done.append(block[k] * scale)
            for c in range(k + 1, 8):
                entry[k, c] = entry[k, c] * scale
            for r in range(k + 1, 8):
                block[r] = block[r] - entry[k, r] * done[k]
                for c in range(r, 8):
                    entry[r, c] = entry[r, c] - entry[k, r] * entry[k, c]
        after = panel + 8
        if after < last:
            old = {(r, c): picked(rows[after + r], base + (after + c)) for r, c in pivots}
            near = [[picked(done[k], base + (after + j)) for j in range(8)] for k in range(8)]
            entry = {
                (r, c): old[r, c] - added([near[k][r] * near[k][c] for k in range(8)])
                for r, c in pivots
            }
            for r in range(8):
                rows[after + r] = rows[after + r] - added([near[k][r] * done[k] for k in range(8)])
            for i in range(after + 8, last):
                rows[i] = rows[i] - added([picked(done[k], base + i) * done[k] for k in range(8)])
        for k in range(8):
            at = (panel + k) * 8
            upper[at : at + 8, :] = jnp.where(inner >= panel + k, done[k], 0.0)


def factorize(grams, upper, used):
    rows = [grams[pl.ds(i, 8, stride=PITCH), :] for i in range(RANK)]
    factorize_rows(rows, 0, HALF, upper)
    side = lanes_left(HALF)
    for pair in range(used):
        top = upper[pl.ds(pair, HALF, stride=8), :]
        turned_top = jnp.transpose(top)
        both = jnp.concatenate([turned_top[HALF:RANK], turned_top[RANK + HALF :]], axis=0)
        taken = exact_dot(both, top)
        at = pair * PITCH + HALF
        grams[at : at + HALF, :] = grams[at : at + HALF, :] - jnp.where(
            side, taken[:HALF], taken[HALF:]
        )
    for i in range(HALF, RANK):
        rows[i] = grams[pl.ds(i, 8, stride=PITCH), :]
    factorize_rows(rows, HALF, RANK, upper)


def visit_order(admissible, leaf, padded_in, blocks, empty):
    padded_in[...] = jnp.full(padded_in.shape, -1, jnp.int32)
    padded_in[0:3, 0 : admissible.shape[1]] = admissible[...]
    level = padded_in[0:1, :]
    row = padded_in[1:2, :]
    column = padded_in[2:3, :]
    low = level <= 2
    base = jnp.where(level == 0, 0, jnp.where(level == 1, CL_DEV, CL_DEV + CL_DEV // 2))
    shift = jnp.where(level == 0, 2, jnp.where(level == 1, 1, 0))
    held = jnp.left_shift(1, shift) - 1
    slot = jnp.where(low, base + jnp.bitwise_and(row, held), level + (SLOTS - 3))
    slot = jnp.where(level < 0, -1, slot)
    side = jnp.minimum(jnp.maximum(jnp.right_shift(column, shift) - leaf + 1, 0), 2)
    place = jnp.where(
        low, side * SLOTS + base + jnp.bitwise_and(column, held), 3 * SLOTS + level - 3
    )
    member = lax.broadcasted_iota(jnp.int32, (16, WIDE), 0) == slot
    ahead = lax.broadcasted_iota(jnp.int32, (WIDE, WIDE), 0) <= lax.broadcasted_iota(
        jnp.int32, (WIDE, WIDE), 1
    )
    member_f = jnp.where(member, 1.0, 0.0).astype(F32)
    rank = jnp.dot(member_f.astype(BF16), jnp.where(ahead, 1.0, 0.0).astype(BF16), preferred_element_type=F32)
    count = jnp.sum(member_f, axis=1, keepdims=True)
    even = jnp.floor((count + 1.0) * 0.5) * 2.0
    even = jnp.broadcast_to(even, (16, WIDE)).astype(BF16)
    below = lax.broadcasted_iota(jnp.int32, (16, 16), 1) < lax.broadcasted_iota(jnp.int32, (16, 16), 0)
    begin = jnp.dot(jnp.where(below, 1.0, 0.0).astype(BF16), even, preferred_element_type=F32)
    at = jnp.sum(jnp.where(member, begin + rank - 1.0, 0.0), axis=0, keepdims=True)
    at = jnp.where(slot < 0, -1.0, at).astype(jnp.int32)
    chosen = lax.broadcasted_iota(jnp.int32, (WIDE, WIDE), 0) == at
    line = lax.broadcasted_iota(jnp.int32, (8, WIDE), 0)
    lane = lax.broadcasted_iota(jnp.int32, (8, WIDE), 1)
    values = jnp.where(line == 0, lane + 1, jnp.where(line == 1, place, jnp.where(line == 2, slot, 0)))
    listed = lax.dot_general(
        values.astype(F32).astype(BF16), jnp.where(chosen, 1.0, 0.0).astype(BF16),
        (((1,), (1,)), ((), ())), preferred_element_type=F32,
    )
    same = jnp.where(listed[2:3] == pltpu.roll(listed, 2, 1)[2:3], 1.0, 0.0)
    last = jnp.where(count > 0.0, (begin + even.astype(F32)) * 0.5 - 1.0, float(empty))
    diagonal = lax.broadcasted_iota(jnp.int32, (16, WIDE), 0) == lax.broadcasted_iota(
        jnp.int32, (16, WIDE), 1
    )
    last = jnp.sum(jnp.where(diagonal, last, 0.0), axis=0, keepdims=True)
    listed = jnp.where(line == 3, same, jnp.where(line == 4, last, listed))
    listed = jnp.where(line == 5, at, listed.astype(jnp.int32))
    limits = (blocks, COLUMNS - 1, ROW_SLOTS - 1, 1, empty, 2 * empty - 1)
    limit = jnp.zeros(line.shape, jnp.int32)
    for k, most in enumerate(limits):
        limit = jnp.where(line == k, most, limit)
    return jnp.minimum(jnp.maximum(listed, 0), limit)


def main_kernel(
    leaves, reps, blocks, chunk, pairs,
    order_in, bottom_in, zero_in, one_in, two_in, three_in, admissible_in, coupling_in,
    projected_to, weights_zero, weights_one, weights_two,
    child, bottom, zero, one, two, three, admissible, coupling, projected, zero_v, one_v, two_v,
    lines, lines_three, page, kids, factors, near, tops, grams, upper,
    padded_in, visits_v, order, row_table, column_left, column_right,
    own, turned, results, snapshots, parts, total,
    fetched, stored, order_sem, send, receive, share_send, share_receive,
):
    me = lax.axis_index("leaf")
    rep = lax.axis_index("rep")
    left = lax.rem(me + leaves - 1, leaves)
    right = lax.rem(me + 1, leaves)
    others = [flipped(me, bits) for bits in range(1, GROUP)]
    start = pl.multiple_of(me // 2 // chunk * chunk, chunk)
    fetches = [
        pltpu.make_async_copy(source, target, fetched.at[k])
        for k, (source, target) in enumerate((
            (bottom_in, bottom), (zero_in, zero), (order_in, child), (one_in, one), (two_in, two),
            (three_in.at[pl.ds(start, chunk)], three), (admissible_in, admissible),
            (coupling_in, coupling),
        ))
    ]
    for fetch in fetches:
        fetch.start()
    barrier = pltpu.get_barrier_semaphore()
    for other in [left, right] + others:
        pl.semaphore_signal(barrier, inc=1, device_id=(other, rep), device_id_type=MESH)
    for step in range(1, reps):
        other = lax.rem(rep + step, reps)
        pl.semaphore_signal(barrier, inc=1, device_id=(me, other), device_id_type=MESH)
    for fetch in fetches[:5]:
        fetch.wait()

    tiles_of(bottom, CL_DEV, lines)
    bottoms = [packed(lines, c) for c in range(CL_DEV)]
    leaf_pairs = [natural_pair(bottoms[c], bottoms[c + 1], page) for c in (0, 2)]
    for k in range(2):
        factors[1, k * RANK : (k + 1) * RANK, :] = leaf_pairs[k].astype(BF16)
    tiles_of(zero, CL_DEV, lines)
    zeros = [packed(lines, c) for c in range(CL_DEV)]
    zero_pairs = [natural_pair(zeros[c], zeros[c + 1], page) for c in (0, 2)]
    tiles_of(one, CL_DEV // 2, lines)
    ones = natural_pair(packed(lines, 0), packed(lines, 1), page)
    tiles_of(two, 1, lines)
    own_two = packed(lines, 0)
    twos = natural_pair(own_two, own_two, page)[:, :RANK]

    for c in range(CL_DEV):
        half = slice(c % 2 * RANK, c % 2 * RANK + RANK)
        image = exact_dot(leaf_pairs[c // 2][:, half], zero_pairs[c // 2][:, half])
        kids[c] = exact_gram(image, image)
    level_one = [kids[child[0, 2 * i]] + kids[child[0, 2 * i + 1]] for i in range(2)]
    near[1, :RANK, :] = jnp.concatenate(level_one, axis=1)
    level_two = 0.0
    for i in range(2):
        transfer = ones[:, i * RANK : (i + 1) * RANK]
        level_two = level_two + exact_gram(transfer, exact_dot(level_one[i], transfer))
    near[1, RANK:, :] = pack(level_two)
    tops[0] = pack(exact_gram(twos, exact_dot(level_two, twos)))

    pl.semaphore_wait(barrier, GROUP + reps)
    copies = []

    def push(source, target, device):
        place = len(copies)
        copy = pltpu.make_async_remote_copy(
            src_ref=source, dst_ref=target, send_sem=send.at[place], recv_sem=receive.at[place],
            device_id=(device, rep), device_id_type=MESH,
        )
        copy.start()
        copies.append(copy)

    for bits in range(1, GROUP):
        push(tops.at[0], tops.at[bits], others[bits - 1])
    push(near.at[1], near.at[2], left)
    push(near.at[1], near.at[0], right)
    push(factors.at[1], factors.at[2], left)
    push(factors.at[1], factors.at[0], right)

    fetches[6].wait()
    visits_v[...] = visit_order(admissible, me, padded_in, blocks, pairs)
    to_scalar = pltpu.make_async_copy(visits_v, order, order_sem)
    to_scalar.start()
    fetches[7].wait()
    own[0] = jnp.zeros((HALF, LANES), BF16)
    turned[0] = jnp.zeros((HALF, LANES), BF16)

    def lay(group, carry):
        first = pl.multiple_of(group * 16, 16)
        x = coupling[pl.ds(first, 16), :].astype(F32)
        for h in range(2):
            for tile in range(HALF):
                at = (h * HALF + tile) * 8
                lines[at : at + 8, :] = x[8 * h : 8 * h + 8, tile * LANES : (tile + 1) * LANES]
        for s in range(16):
            block = lines[pl.ds(s // 8 * 256 + s % 8, HALF, stride=8), :]
            own[first + s + 1] = block.astype(BF16)
            turned[first + s + 1] = swap(block).astype(BF16)
        return carry

    lax.fori_loop(0, blocks // 16, lay, 0, unroll=2)

    fetches[5].wait()
    tiles_of(three, chunk, lines_three)
    place = lax.rem(me // 2, chunk)
    threes = []
    for u in range(GROUP // 2):
        matrix = packed(lines_three, flipped(place, u))
        threes.append(natural_pair(matrix, matrix, page)[:, :RANK])
    for copy in copies[: GROUP - 1]:
        copy.wait_recv()
    level_three, lifted = [], []
    for u in range(GROUP // 2):
        gram = unpack(tops[2 * u] + tops[2 * u + 1])
        level_three.append(gram)
        lifted.append(exact_gram(threes[u], exact_dot(gram, threes[u])))
    level_four = [lifted[0] + lifted[1], lifted[2] + lifted[3]]
    for copy in copies[GROUP - 1 :]:
        copy.wait_recv()
    for side in range(3):
        grams[side * PITCH : side * PITCH + RANK, :] = near[side, :RANK, :]
    side_two = [unpack(near[side, RANK:, :]) for side in range(3)]
    rest = side_two + [level_three[0], level_three[1], level_four[0], level_four[1], level_four[1]]
    for k in range(4):
        at = (3 + k) * PITCH
        grams[at : at + RANK, :] = jnp.concatenate([rest[2 * k], rest[2 * k + 1]], axis=1)
    grams[7 * PITCH : 7 * PITCH + RANK, :] = near[1, :RANK, :]

    side = lanes_left(HALF)
    side_full = lanes_left(RANK)
    lane = lax.broadcasted_iota(jnp.int32, (RANK, LANES), 1)
    inner = jnp.where(lane < RANK, lane, lane - RANK)
    spread = jnp.where(inner < HALF, 2 * inner, 2 * inner - (RANK - 1)) + (lane - inner)

    factorize(grams, upper, 7)

    def put_column(where, left, right):
        column_left[where] = left.astype(BF16)
        column_right[where] = right.astype(BF16)

    def put_columns(first, second, names):
        flipped_all = jnp.transpose(jnp.concatenate([first, second], axis=0))
        for half in range(2):
            part = flipped_all[half * RANK : (half + 1) * RANK]
            other = swap(part)
            if names[half] is not None:
                put_column(names[half], jnp.where(side_full, part, 0.0), jnp.where(side_full, 0.0, other))
            if names[2 + half] is not None:
                put_column(names[2 + half], jnp.where(side_full, other, 0.0), jnp.where(side_full, 0.0, part))

    def put_rows(even, odd, names):
        x = picked(jnp.concatenate([even, odd], axis=0), spread)
        if names[0] is not None:
            row_table[names[0]] = x.astype(BF16)
        if names[1] is not None:
            row_table[names[1]] = swap(x).astype(BF16)

    for near_by in range(3):
        first = factors[near_by, :RANK, :].astype(F32)
        second = factors[near_by, RANK:, :].astype(F32)
        put_columns(first, second, [near_by * SLOTS + c for c in (0, 1, 2, 3)])
        if near_by == 1:
            for k, x in enumerate((first, second)):
                lines[k * RANK : (k + 1) * RANK, :] = x
                put_rows(
                    lines[pl.ds(k * RANK, HALF, stride=2), :],
                    lines[pl.ds(k * RANK + 1, HALF, stride=2), :],
                    (2 * k, 2 * k + 1),
                )
    column_names = [
        (4, 5), (SLOTS + 4, SLOTS + 5), (2 * SLOTS + 4, 2 * SLOTS + 5), (6, SLOTS + 6),
        (2 * SLOTS + 6, None), (3 * SLOTS, None), (3 * SLOTS + 1, None), (None, None),
    ]
    for k in range(0, 8, 2):
        put_columns(
            upper[pl.ds(k, RANK, stride=8), :], upper[pl.ds(k + 1, RANK, stride=8), :],
            column_names[k] + column_names[k + 1],
        )
    for k, names in ((1, (4, 5)), (3, (None, 6)), (4, (None, 7)), (5, (None, 8))):
        put_rows(upper[pl.ds(k, HALF, stride=16), :], upper[pl.ds(8 + k, HALF, stride=16), :], names)

    snapshots[pairs] = jnp.zeros((RANK, LANES), F32)
    to_scalar.wait()

    def visits(step, carry):
        places = [step * BATCH + k for k in range(BATCH)]
        halves = []
        for pair in places:
            a, b = order[0, 2 * pair], order[0, 2 * pair + 1]
            both = jnp.concatenate(
                [jnp.where(side, own[a], turned[b]), jnp.where(side, turned[a], own[b])], axis=0
            )
            slot = order[2, 2 * pair]
            halves.append(
                jnp.dot(row_table[slot][:, :RANK], both, preferred_element_type=F32).astype(BF16)
            )
        products = []
        for pair, half in zip(places, halves):
            columns = jnp.concatenate(
                [column_left[order[1, 2 * pair]], column_right[order[1, 2 * pair + 1]]], axis=0
            )
            products.append(jnp.dot(half, columns, preferred_element_type=F32))
        terms = []
        for product in products:
            rounded = product.astype(BF16)
            terms.append(lax.dot_general(
                rounded, rounded, (((1,), (1,)), ((), ())), preferred_element_type=F32
            ))
        for pair, result in zip(places, products):
            top, bottom_half = result[:HALF], result[HALF:]
            results[2 * pair] = jnp.where(side, top, swap(bottom_half))
            results[2 * pair + 1] = jnp.where(side, swap(top), bottom_half)
        for pair, term in zip(places, terms):
            carry = carry * order[3, 2 * pair].astype(F32) + term
            snapshots[pair, :, :RANK] = carry
        return carry

    lax.fori_loop(0, pairs // BATCH, visits, jnp.zeros((RANK, RANK), F32))

    gather = jnp.where(inner % 2 == 0, inner // 2, HALF + inner // 2)
    for s in range(SLOTS):
        x = picked(snapshots[order[4, s]], gather)
        part = jnp.where(side, x[:HALF], x[HALF:]) * (1.0 / RANK)
        parts[rep, s * HALF : (s + 1) * HALF, :] = part.astype(BF16)
    shares = []
    for step in range(1, reps):
        copy = pltpu.make_async_remote_copy(
            src_ref=parts.at[rep], dst_ref=parts.at[rep],
            send_sem=share_send.at[step - 1], recv_sem=share_receive.at[step - 1],
            device_id=(me, lax.rem(rep + step, reps)), device_id_type=MESH,
        )
        copy.start()
        shares.append(copy)

    def store_of(group):
        span = pl.ds(pl.multiple_of(group * 16, 16), 16)
        return pltpu.make_async_copy(projected.at[span], projected_to.at[span], stored.at[group])

    def write(group, carry):
        first = pl.multiple_of(group * 16, 16)
        for s in range(16):
            lines[s * APART : s * APART + HALF, :] = results[order[5, first + s]]
        for tile in range(HALF):
            x = jnp.concatenate(
                [
                    lines[pl.ds(tile, 8, stride=APART), :],
                    lines[pl.ds(tile + 8 * APART, 8, stride=APART), :],
                ],
                axis=0,
            )
            projected[pl.ds(first, 16), tile * LANES : (tile + 1) * LANES] = x.astype(BF16)
        store_of(group).start()
        return carry

    groups = blocks // 16
    lax.fori_loop(0, groups, write, 0)
    for copy in shares:
        copy.wait_recv()
    added_up = parts[0].astype(F32)
    for k in range(1, reps):
        added_up = added_up + parts[k].astype(F32)
    for s in range(SLOTS):
        total[s * APART : s * APART + HALF, :] = added_up[s * HALF : (s + 1) * HALF]
    for tile in range(HALF):
        span = slice(tile * LANES, (tile + 1) * LANES)
        zero_v[:, span] = total[pl.ds(tile, CL_DEV, stride=APART), :]
        one_v[:, span] = total[pl.ds(tile + CL_DEV * APART, CL_DEV // 2, stride=APART), :]
        at = tile + (SLOTS - 1) * APART
        two_v[:, span] = total[at : at + 1, :]
    stores = [
        pltpu.make_async_copy(source, target, stored.at[groups + k])
        for k, (source, target) in enumerate(
            ((zero_v, weights_zero), (one_v, weights_one), (two_v, weights_two))
        )
    ]
    for store in stores:
        store.start()
    for copy in copies + shares:
        copy.wait_send()
    for store in stores + [store_of(group) for group in range(groups)]:
        store.wait()


def main_call(leaves, reps, order, bottom, zero, one, two, three, admissible, coupling):
    chunk = min(8, three.shape[0])
    blocks = coupling.shape[0]
    pairs = (blocks + ROW_SLOTS) // 2
    pairs = -(-pairs // BATCH) * BATCH
    hbm = pl.BlockSpec(memory_space=pltpu.HBM)
    small = [jax.ShapeDtypeStruct((count, FLAT), F32) for count in (CL_DEV, CL_DEV // 2, 1)]
    count = GROUP + 3
    whole = [bottom, zero, one, two]
    return pl.pallas_call(
        functools.partial(main_kernel, leaves, reps, blocks, chunk, pairs),
        out_shape=[jax.ShapeDtypeStruct((blocks, FLAT), BF16)] + small,
        in_specs=[hbm] * 8,
        out_specs=[hbm] * 4,
        scratch_shapes=[
            pltpu.SMEM(order.shape, jnp.int32),
            *[pltpu.VMEM(x.shape, x.dtype) for x in whole],
            pltpu.VMEM((chunk, FLAT), F32),
            pltpu.VMEM(admissible.shape, jnp.int32),
            pltpu.VMEM(coupling.shape, BF16),
            pltpu.VMEM(coupling.shape, BF16),
            *[pltpu.VMEM(x.shape, F32) for x in small],
            pltpu.VMEM((640, LANES), F32),
            pltpu.VMEM((HALF * 8, LANES), F32),
            pltpu.VMEM((RANK, LANES), F32),
            pltpu.VMEM((CL_DEV, RANK, RANK), F32),
            pltpu.VMEM((3, LANES, LANES), BF16),
            pltpu.VMEM((3, RANK + HALF, LANES), F32),
            pltpu.VMEM((GROUP, HALF, LANES), F32),
            pltpu.VMEM((8 * PITCH, LANES), F32),
            pltpu.VMEM((8 * RANK, LANES), F32),
            pltpu.VMEM((8, WIDE), jnp.int32),
            pltpu.VMEM((8, WIDE), jnp.int32),
            pltpu.SMEM((8, WIDE), jnp.int32),
            pltpu.VMEM((ROW_SLOTS, RANK, LANES), BF16),
            pltpu.VMEM((COLUMNS, RANK, LANES), BF16),
            pltpu.VMEM((COLUMNS, RANK, LANES), BF16),
            pltpu.VMEM((blocks + 1, HALF, LANES), BF16),
            pltpu.VMEM((blocks + 1, HALF, LANES), BF16),
            pltpu.VMEM((2 * pairs, HALF, LANES), F32),
            pltpu.VMEM((pairs + 1, RANK, LANES), F32),
            pltpu.VMEM((reps, SLOTS * HALF, LANES), BF16),
            pltpu.VMEM((SLOTS * APART, LANES), F32),
            pltpu.SemaphoreType.DMA((8,)),
            pltpu.SemaphoreType.DMA((blocks // 16 + 3,)),
            pltpu.SemaphoreType.DMA,
            pltpu.SemaphoreType.DMA((count,)),
            pltpu.SemaphoreType.DMA((count,)),
            pltpu.SemaphoreType.DMA((reps - 1,)),
            pltpu.SemaphoreType.DMA((reps - 1,)),
        ],
        compiler_params=pltpu.CompilerParams(
            collective_id=0, has_side_effects=True, vmem_limit_bytes=60 * MIB
        ),
        name="upsweep_and_blocks",
    )(order, bottom, zero, one, two, three, admissible, coupling)


def deliver_kernel(parts, *refs):
    count = len(refs) // 3
    sources, targets, held = refs[:count], refs[count : 2 * count], refs[2 * count : 3 * count]
    came, went = refs[3 * count :]
    rows = sources[0].shape[0] // parts
    spans = [(0, pl.ds(k * rows, rows)) for k in range(parts)]
    spans += [(k, pl.ds(0, sources[k].shape[0])) for k in range(1, count)]
    reads = [
        pltpu.make_async_copy(sources[k].at[span], held[k].at[span], came.at[n])
        for n, (k, span) in enumerate(spans)
    ]
    writes = [
        pltpu.make_async_copy(held[k].at[span], targets[k].at[span], went.at[n])
        for n, (k, span) in enumerate(spans)
    ]
    for read in reads:
        read.start()
    for read, write in zip(reads, writes):
        read.wait()
        write.start()
    for write in writes:
        write.wait()


def deliver_call(*arrays):
    hbm = pl.BlockSpec(memory_space=pltpu.HBM)
    parts = 4
    moves = len(arrays) - 1 + parts
    return pl.pallas_call(
        functools.partial(deliver_kernel, parts),
        out_shape=[jax.ShapeDtypeStruct(x.shape, x.dtype) for x in arrays],
        in_specs=[hbm] * len(arrays),
        out_specs=[hbm] * len(arrays),
        scratch_shapes=[pltpu.VMEM(x.shape, x.dtype) for x in arrays]
        + [pltpu.SemaphoreType.DMA((moves,))] * 2,
        compiler_params=pltpu.CompilerParams(vmem_limit_bytes=60 * MIB),
        name="deliver",
    )(*arrays)


def local(leaves, reps, bottom, zero, one, two, three, order, coupling, admissible):
    return tuple(deliver_call(
        *main_call(leaves, reps, order, bottom, zero, one, two, three, admissible, coupling)
    ))


def solution(mesh):
    return jax.shard_map(
        functools.partial(local, mesh.shape["leaf"], mesh.shape["rep"]),
        mesh=mesh,
        in_specs=(
            P("leaf", None),
            P("leaf", None),
            P("leaf", None),
            P("leaf", None),
            P(),
            P("leaf", None),
            P(("leaf", "rep"), None),
            P(None, ("leaf", "rep")),
        ),
        out_specs=(P(("leaf", "rep"), None), P("leaf", None), P("leaf", None), P("leaf", None)),
        check_vma=False,
    )
```

```python
import functools

import jax
import jax.numpy as jnp
from jax import lax
from jax.experimental import pallas as pl
from jax.experimental.pallas import tpu as pltpu
from jax.sharding import PartitionSpec as P

RANK = 64
HALF = 32
LANES = 128
FLAT = RANK * RANK
CL_DEV = 4
SLOTS = 7
ROW_SLOTS = 9
COLUMNS = 3 * SLOTS + 2
GROUP = 8
MESH = pl.DeviceIdType.MESH
F32 = jnp.float32
BF16 = jnp.bfloat16
EXACT = lax.Precision.HIGHEST
WIDE = 256
PITCH = 72
APART = 40
MIB = 1024 * 1024


def lanes_left(rows):
    return lax.broadcasted_iota(jnp.int32, (rows, LANES), 1) < RANK


def swap(x):
    return pltpu.roll(x, RANK, 1)


def exact_dot(a, b):
    return jnp.dot(a, b, precision=EXACT, preferred_element_type=F32)


def exact_gram(a, b):
    return lax.dot_general(a, b, (((0,), (0,)), ((), ())), precision=EXACT, preferred_element_type=F32)


def flipped(index, bits):
    result = index
    for place in range(3):
        if bits >> place & 1:
            result = result + (1 - 2 * (index // (1 << place) % 2)) * (1 << place)
    return result


def tiles_of(flat, rows, lines):
    for tile in range(HALF):
        lines[tile * 8 : tile * 8 + rows, :] = flat[:, tile * LANES : (tile + 1) * LANES]


def packed(lines, which):
    return lines[pl.ds(which, HALF, stride=8), :]


def natural_pair(left, right, page):
    side = lanes_left(HALF)
    page[pl.ds(0, HALF, stride=2), :] = jnp.where(side, left, swap(right))
    page[pl.ds(1, HALF, stride=2), :] = jnp.where(side, swap(left), right)
    return page[...]


def pack(x):
    return jnp.concatenate([x[:HALF], x[HALF:]], axis=1)


def unpack(x):
    return jnp.concatenate([x[:, :RANK], x[:, RANK:]], axis=0)


def picked(x, index):
    return jnp.take_along_axis(x, index, axis=1, mode="promise_in_bounds")


def added(terms):
    while len(terms) > 1:
        terms = [sum(terms[k + 1 : k + 2], terms[k]) for k in range(0, len(terms), 2)]
    return terms[0]


def factorize_rows(rows, first, last, upper):
    lane = lax.broadcasted_iota(jnp.int32, (8, LANES), 1)
    base = jnp.where(lane < RANK, 0, RANK)
    inner = lane - base
    pivots = [(r, c) for r in range(8) for c in range(r, 8)]
    entry = {(r, c): picked(rows[first + r], base + (first + c)) for r, c in pivots}
    for panel in range(first, last, 8):
        block = rows[panel : panel + 8]
        done = []
        for k in range(8):
            scale = lax.rsqrt(entry[k, k])
            done.append(block[k] * scale)
            for c in range(k + 1, 8):
                entry[k, c] = entry[k, c] * scale
            for r in range(k + 1, 8):
                block[r] = block[r] - entry[k, r] * done[k]
                for c in range(r, 8):
                    entry[r, c] = entry[r, c] - entry[k, r] * entry[k, c]
        after = panel + 8
        if after < last:
            old = {(r, c): picked(rows[after + r], base + (after + c)) for r, c in pivots}
            near = [[picked(done[k], base + (after + j)) for j in range(8)] for k in range(8)]
            entry = {
                (r, c): old[r, c] - added([near[k][r] * near[k][c] for k in range(8)])
                for r, c in pivots
            }
            for r in range(8):
                rows[after + r] = rows[after + r] - added([near[k][r] * done[k] for k in range(8)])
            for i in range(after + 8, last):
                rows[i] = rows[i] - added([picked(done[k], base + i) * done[k] for k in range(8)])
        for k in range(8):
            at = (panel + k) * 8
            upper[at : at + 8, :] = jnp.where(inner >= panel + k, done[k], 0.0)


def factorize(grams, upper, used):
    rows = [grams[pl.ds(i, 8, stride=PITCH), :] for i in range(RANK)]
    factorize_rows(rows, 0, HALF, upper)
    side = lanes_left(HALF)
    for pair in range(used):
        top = upper[pl.ds(pair, HALF, stride=8), :]
        turned_top = jnp.transpose(top)
        both = jnp.concatenate([turned_top[HALF:RANK], turned_top[RANK + HALF :]], axis=0)
        taken = exact_dot(both, top)
        at = pair * PITCH + HALF
        grams[at : at + HALF, :] = grams[at : at + HALF, :] - jnp.where(
            side, taken[:HALF], taken[HALF:]
        )
    for i in range(HALF, RANK):
        rows[i] = grams[pl.ds(i, 8, stride=PITCH), :]
    factorize_rows(rows, HALF, RANK, upper)


def visit_order(admissible, leaf, padded_in, blocks, empty):
    padded_in[...] = jnp.full(padded_in.shape, -1, jnp.int32)
    padded_in[0:3, 0 : admissible.shape[1]] = admissible[...]
    level = padded_in[0:1, :]
    row = padded_in[1:2, :]
    column = padded_in[2:3, :]
    low = level <= 2
    base = jnp.where(level == 0, 0, jnp.where(level == 1, CL_DEV, CL_DEV + CL_DEV // 2))
    shift = jnp.where(level == 0, 2, jnp.where(level == 1, 1, 0))
    held = jnp.left_shift(1, shift) - 1
    slot = jnp.where(low, base + jnp.bitwise_and(row, held), level + (SLOTS - 3))
    slot = jnp.where(level < 0, -1, slot)
    side = jnp.minimum(jnp.maximum(jnp.right_shift(column, shift) - leaf + 1, 0), 2)
    place = jnp.where(
        low, side * SLOTS + base + jnp.bitwise_and(column, held), 3 * SLOTS + level - 3
    )
    member = lax.broadcasted_iota(jnp.int32, (16, WIDE), 0) == slot
    ahead = lax.broadcasted_iota(jnp.int32, (WIDE, WIDE), 0) <= lax.broadcasted_iota(
        jnp.int32, (WIDE, WIDE), 1
    )
    member_f = jnp.where(member, 1.0, 0.0).astype(F32)
    rank = jnp.dot(member_f.astype(BF16), jnp.where(ahead, 1.0, 0.0).astype(BF16), preferred_element_type=F32)
    count = jnp.sum(member_f, axis=1, keepdims=True)
    even = jnp.floor((count + 3.0) * 0.25) * 4.0
    even = jnp.broadcast_to(even, (16, WIDE)).astype(BF16)
    below = lax.broadcasted_iota(jnp.int32, (16, 16), 1) < lax.broadcasted_iota(jnp.int32, (16, 16), 0)
    begin = jnp.dot(jnp.where(below, 1.0, 0.0).astype(BF16), even, preferred_element_type=F32)
    at = jnp.sum(jnp.where(member, begin + rank - 1.0, 0.0), axis=0, keepdims=True)
    at = jnp.where(slot < 0, -1.0, at).astype(jnp.int32)
    chosen = lax.broadcasted_iota(jnp.int32, (WIDE, WIDE), 0) == at
    line = lax.broadcasted_iota(jnp.int32, (8, WIDE), 0)
    lane = lax.broadcasted_iota(jnp.int32, (8, WIDE), 1)
    values = jnp.where(line == 0, lane + 1, jnp.where(line == 1, place, jnp.where(line == 2, slot, 0)))
    listed = lax.dot_general(
        values.astype(F32).astype(BF16), jnp.where(chosen, 1.0, 0.0).astype(BF16),
        (((1,), (1,)), ((), ())), preferred_element_type=F32,
    )
    same = jnp.where(listed[2:3] == pltpu.roll(listed, 4, 1)[2:3], 1.0, 0.0)
    last = jnp.where(count > 0.0, (begin + even.astype(F32)) * 0.25 - 1.0, float(empty))
    diagonal = lax.broadcasted_iota(jnp.int32, (16, WIDE), 0) == lax.broadcasted_iota(
        jnp.int32, (16, WIDE), 1
    )
    last = jnp.sum(jnp.where(diagonal, last, 0.0), axis=0, keepdims=True)
    listed = jnp.where(line == 3, same, jnp.where(line == 4, last, listed))
    listed = jnp.where(line == 5, at, listed.astype(jnp.int32))
    limits = (blocks, COLUMNS - 1, ROW_SLOTS - 1, 1, empty, 4 * empty - 1)
    limit = jnp.zeros(line.shape, jnp.int32)
    for k, most in enumerate(limits):
        limit = jnp.where(line == k, most, limit)
    return jnp.minimum(jnp.maximum(listed, 0), limit)


def main_kernel(
    leaves, reps, blocks, chunk, fours,
    order_in, bottom_in, zero_in, one_in, two_in, three_in, admissible_in, coupling_in,
    projected_to, parts_to,
    child, bottom, zero, one, two, three, admissible, coupling, projected,
    lines, lines_three, page, kids, factors, near, tops, grams, upper,
    padded_in, visits_v, order, row_table, column_left, column_right,
    own, turned, results, snapshots, share,
    fetched, stored, order_sem, send, receive, share_send, share_receive,
):
    me = lax.axis_index("leaf")
    rep = lax.axis_index("rep")
    left = lax.rem(me + leaves - 1, leaves)
    right = lax.rem(me + 1, leaves)
    others = [flipped(me, bits) for bits in range(1, GROUP)]
    start = pl.multiple_of(me // 2 // chunk * chunk, chunk)
    fetches = [
        pltpu.make_async_copy(source, target, fetched.at[k])
        for k, (source, target) in enumerate((
            (bottom_in, bottom), (zero_in, zero), (order_in, child), (one_in, one), (two_in, two),
            (three_in.at[pl.ds(start, chunk)], three), (admissible_in, admissible),
            (coupling_in, coupling),
        ))
    ]
    for fetch in fetches:
        fetch.start()
    barrier = pltpu.get_barrier_semaphore()
    for other in others:
        pl.semaphore_signal(barrier, inc=1, device_id=(other, rep), device_id_type=MESH)

    @pl.when(me > 0)
    def _():
        pl.semaphore_signal(barrier, inc=1, device_id=(left, rep), device_id_type=MESH)

    @pl.when(me < leaves - 1)
    def _():
        pl.semaphore_signal(barrier, inc=1, device_id=(right, rep), device_id_type=MESH)

    for step in range(1, reps):
        other = lax.rem(rep + step, reps)
        pl.semaphore_signal(barrier, inc=1, device_id=(me, other), device_id_type=MESH)
    for fetch in fetches[:7]:
        fetch.wait()

    tiles_of(bottom, CL_DEV, lines)
    bottoms = [packed(lines, c) for c in range(CL_DEV)]
    leaf_pairs = [natural_pair(bottoms[c], bottoms[c + 1], page) for c in (0, 2)]
    for k in range(2):
        factors[1, k * RANK : (k + 1) * RANK, :] = leaf_pairs[k].astype(BF16)
    tiles_of(zero, CL_DEV, lines)
    zeros = [packed(lines, c) for c in range(CL_DEV)]
    zero_pairs = [natural_pair(zeros[c], zeros[c + 1], page) for c in (0, 2)]
    tiles_of(one, CL_DEV // 2, lines)
    ones = natural_pair(packed(lines, 0), packed(lines, 1), page)
    tiles_of(two, 1, lines)
    own_two = packed(lines, 0)
    twos = natural_pair(own_two, own_two, page)[:, :RANK]

    tiles_of(three, chunk, lines_three)
    place = lax.rem(me // 2, chunk)
    threes = []
    for u in range(GROUP // 2):
        matrix = packed(lines_three, flipped(place, u))
        threes.append(natural_pair(matrix, matrix, page)[:, :RANK])
    visits_v[...] = visit_order(admissible, me, padded_in, blocks, fours)

    for c in range(CL_DEV):
        half = slice(c % 2 * RANK, c % 2 * RANK + RANK)
        image = exact_dot(leaf_pairs[c // 2][:, half], zero_pairs[c // 2][:, half])
        kids[c] = exact_gram(image, image)
    level_one = [kids[child[0, 2 * i]] + kids[child[0, 2 * i + 1]] for i in range(2)]
    near[1, :RANK, :] = jnp.concatenate(level_one, axis=1)
    level_two = 0.0
    for i in range(2):
        transfer = ones[:, i * RANK : (i + 1) * RANK]
        level_two = level_two + exact_gram(transfer, exact_dot(level_one[i], transfer))
    near[1, RANK:, :] = pack(level_two)

    at_edge = (me == 0) | (me == leaves - 1)
    pl.when(at_edge)(lambda: pl.semaphore_wait(barrier, GROUP + reps - 1))
    pl.when(jnp.logical_not(at_edge))(lambda: pl.semaphore_wait(barrier, GROUP + reps))
    copies = []

    def push(source, target, device):
        place = len(copies)
        copy = pltpu.make_async_remote_copy(
            src_ref=source, dst_ref=target, send_sem=send.at[place], recv_sem=receive.at[place],
            device_id=(device, rep), device_id_type=MESH,
        )
        copies.append(copy)
        return copy

    push(near.at[1], near.at[2], left)
    push(near.at[1], near.at[0], right)
    pl.when(me > 0)(copies[0].start)
    pl.when(me < leaves - 1)(copies[1].start)
    tops[0] = pack(exact_gram(twos, exact_dot(level_two, twos)))

    to_scalar = pltpu.make_async_copy(visits_v, order, order_sem)
    to_scalar.start()
    for bits in range(1, GROUP):
        push(tops.at[0], tops.at[bits], others[bits - 1]).start()
    push(factors.at[1], factors.at[2], left)
    push(factors.at[1], factors.at[0], right)
    pl.when(me > 0)(copies[-2].start)
    pl.when(me < leaves - 1)(copies[-1].start)

    fetches[7].wait()
    own[0] = jnp.zeros((HALF, LANES), BF16)
    turned[0] = jnp.zeros((HALF, LANES), BF16)

    def lay(group, carry):
        first = pl.multiple_of(group * 16, 16)
        x = coupling[pl.ds(first, 16), :].astype(F32)
        for h in range(2):
            for tile in range(HALF):
                at = (h * HALF + tile) * 8
                lines[at : at + 8, :] = x[8 * h : 8 * h + 8, tile * LANES : (tile + 1) * LANES]
        for s in range(16):
            block = lines[pl.ds(s // 8 * 256 + s % 8, HALF, stride=8), :]
            own[first + s + 1] = block.astype(BF16)
            turned[first + s + 1] = swap(block).astype(BF16)
        return carry

    lax.fori_loop(0, blocks // 16, lay, 0, unroll=2)

    for copy in copies[2 : GROUP + 1]:
        copy.wait_recv()
    level_three, lifted = [], []
    for u in range(GROUP // 2):
        gram = unpack(tops[2 * u] + tops[2 * u + 1])
        level_three.append(gram)
        lifted.append(exact_gram(threes[u], exact_dot(gram, threes[u])))
    level_four = [lifted[0] + lifted[1], lifted[2] + lifted[3]]
    pl.when(me < leaves - 1)(copies[0].wait_recv)
    pl.when(me > 0)(copies[1].wait_recv)

    @pl.when(me == 0)
    def _():
        near[0] = near[1]
        factors[0] = factors[1]

    @pl.when(me == leaves - 1)
    def _():
        near[2] = near[1]
        factors[2] = factors[1]

    for side in range(3):
        grams[side * PITCH : side * PITCH + RANK, :] = near[side, :RANK, :]
    side_two = [unpack(near[side, RANK:, :]) for side in range(3)]
    rest = side_two + [level_three[0], level_three[1], level_four[0], level_four[1], level_four[1]]
    for k in range(4):
        at = (3 + k) * PITCH
        grams[at : at + RANK, :] = jnp.concatenate([rest[2 * k], rest[2 * k + 1]], axis=1)
    grams[7 * PITCH : 7 * PITCH + RANK, :] = near[1, :RANK, :]

    side = lanes_left(HALF)
    side_full = lanes_left(RANK)
    lane = lax.broadcasted_iota(jnp.int32, (RANK, LANES), 1)
    inner = jnp.where(lane < RANK, lane, lane - RANK)
    spread = jnp.where(inner < HALF, 2 * inner, 2 * inner - (RANK - 1)) + (lane - inner)

    factorize(grams, upper, 7)
    pl.when(me < leaves - 1)(copies[-2].wait_recv)
    pl.when(me > 0)(copies[-1].wait_recv)

    def put_column(where, left, right):
        column_left[where] = left.astype(BF16)
        column_right[where] = right.astype(BF16)

    def put_columns(first, second, names):
        flipped_all = jnp.transpose(jnp.concatenate([first, second], axis=0))
        for half in range(2):
            part = flipped_all[half * RANK : (half + 1) * RANK]
            other = swap(part)
            if names[half] is not None:
                put_column(names[half], jnp.where(side_full, part, 0.0), jnp.where(side_full, 0.0, other))
            if names[2 + half] is not None:
                put_column(names[2 + half], jnp.where(side_full, other, 0.0), jnp.where(side_full, 0.0, part))

    def put_rows(even, odd, names):
        x = picked(jnp.concatenate([even, odd], axis=0), spread)
        if names[0] is not None:
            row_table[names[0]] = x.astype(BF16)
        if names[1] is not None:
            row_table[names[1]] = swap(x).astype(BF16)

    for near_by in range(3):
        first = factors[near_by, :RANK, :].astype(F32)
        second = factors[near_by, RANK:, :].astype(F32)
        put_columns(first, second, [near_by * SLOTS + c for c in (0, 1, 2, 3)])
        if near_by == 1:
            for k, x in enumerate((first, second)):
                lines[k * RANK : (k + 1) * RANK, :] = x
                put_rows(
                    lines[pl.ds(k * RANK, HALF, stride=2), :],
                    lines[pl.ds(k * RANK + 1, HALF, stride=2), :],
                    (2 * k, 2 * k + 1),
                )
    column_names = [
        (4, 5), (SLOTS + 4, SLOTS + 5), (2 * SLOTS + 4, 2 * SLOTS + 5), (6, SLOTS + 6),
        (2 * SLOTS + 6, None), (3 * SLOTS, None), (3 * SLOTS + 1, None), (None, None),
    ]
    for k in range(0, 8, 2):
        put_columns(
            upper[pl.ds(k, RANK, stride=8), :], upper[pl.ds(k + 1, RANK, stride=8), :],
            column_names[k] + column_names[k + 1],
        )
    for k, names in ((1, (4, 5)), (3, (None, 6)), (4, (None, 7)), (5, (None, 8))):
        put_rows(upper[pl.ds(k, HALF, stride=16), :], upper[pl.ds(8 + k, HALF, stride=16), :], names)

    snapshots[fours] = jnp.zeros((RANK, LANES), F32)
    to_scalar.wait()

    halves = []
    for four in range(fours):
        sides = []
        for k in range(4 * four, 4 * four + 4, 2):
            a, b = order[0, k], order[0, k + 1]
            sides.append(jnp.concatenate(
                [jnp.where(side, own[a], turned[b]), jnp.where(side, turned[a], own[b])], axis=0
            ))
        row = row_table[order[2, 4 * four]][:, :RANK]
        halves.append(
            jnp.dot(row, jnp.concatenate(sides, axis=1), preferred_element_type=F32).astype(BF16)
        )
    products = []
    for four, half in enumerate(halves):
        for k in range(2):
            at = 4 * four + 2 * k
            columns = jnp.concatenate(
                [column_left[order[1, at]], column_right[order[1, at + 1]]], axis=0
            )
            span = slice(k * LANES, (k + 1) * LANES)
            products.append(jnp.dot(half[:, span], columns, preferred_element_type=F32))
    terms = []
    for four in range(fours):
        rounded = jnp.concatenate(products[2 * four : 2 * four + 2], axis=1).astype(BF16)
        terms.append(lax.dot_general(
            rounded, rounded, (((1,), (1,)), ((), ())), preferred_element_type=F32
        ))
    for pair, result in enumerate(products):
        top, bottom_half = result[:HALF], result[HALF:]
        results[2 * pair] = jnp.where(side, top, swap(bottom_half))
        results[2 * pair + 1] = jnp.where(side, swap(top), bottom_half)
    running = jnp.zeros((RANK, RANK), F32)
    for four, term in enumerate(terms):
        running = running * order[3, 4 * four].astype(F32) + term
        snapshots[four, :, :RANK] = running

    gather = jnp.where(inner % 2 == 0, inner // 2, HALF + inner // 2)
    for s in range(SLOTS):
        x = picked(snapshots[order[4, s]], gather)
        part = jnp.where(side, x[:HALF], x[HALF:]) * (1.0 / RANK)
        share[s * HALF : (s + 1) * HALF, :] = part.astype(BF16)
    shares = []
    for step in range(1, reps):
        copy = pltpu.make_async_remote_copy(
            src_ref=share, dst_ref=parts_to.at[rep],
            send_sem=share_send.at[step - 1], recv_sem=share_receive.at[step - 1],
            device_id=(me, lax.rem(rep + step, reps)), device_id_type=MESH,
        )
        copy.start()
        shares.append(copy)

    own_share = pltpu.make_async_copy(share, parts_to.at[rep], stored.at[blocks // 16])
    own_share.start()

    def store_of(group):
        span = pl.ds(pl.multiple_of(group * 16, 16), 16)
        return pltpu.make_async_copy(projected.at[span], projected_to.at[span], stored.at[group])

    def write(group, carry):
        first = pl.multiple_of(group * 16, 16)
        for s in range(16):
            lines[s * APART : s * APART + HALF, :] = results[order[5, first + s]]
        for tile in range(HALF):
            x = jnp.concatenate(
                [
                    lines[pl.ds(tile, 8, stride=APART), :],
                    lines[pl.ds(tile + 8 * APART, 8, stride=APART), :],
                ],
                axis=0,
            )
            projected[pl.ds(first, 16), tile * LANES : (tile + 1) * LANES] = x.astype(BF16)
        store_of(group).start()
        return carry

    groups = blocks // 16
    lax.fori_loop(0, groups, write, 0)
    for copy in shares:
        copy.wait_recv()
    for copy in copies[2 : GROUP + 1] + shares:
        copy.wait_send()
    pl.when(me > 0)(copies[0].wait_send)
    pl.when(me < leaves - 1)(copies[1].wait_send)
    pl.when(me > 0)(copies[-2].wait_send)
    pl.when(me < leaves - 1)(copies[-1].wait_send)
    own_share.wait()
    for group in range(groups):
        store_of(group).wait()


def main_call(leaves, reps, order, bottom, zero, one, two, three, admissible, coupling):
    chunk = min(8, three.shape[0])
    blocks = coupling.shape[0]
    fours = (blocks + 3 * ROW_SLOTS) // 4
    hbm = pl.BlockSpec(memory_space=pltpu.HBM)
    count = GROUP + 3
    whole = [bottom, zero, one, two]
    return pl.pallas_call(
        functools.partial(main_kernel, leaves, reps, blocks, chunk, fours),
        out_shape=[
            jax.ShapeDtypeStruct((blocks, FLAT), BF16),
            jax.ShapeDtypeStruct((reps, SLOTS * HALF, LANES), BF16),
        ],
        in_specs=[hbm] * 8,
        out_specs=[hbm] * 2,
        scratch_shapes=[
            pltpu.SMEM(order.shape, jnp.int32),
            *[pltpu.VMEM(x.shape, x.dtype) for x in whole],
            pltpu.VMEM((chunk, FLAT), F32),
            pltpu.VMEM(admissible.shape, jnp.int32),
            pltpu.VMEM(coupling.shape, BF16),
            pltpu.VMEM(coupling.shape, BF16),
            pltpu.VMEM((640, LANES), F32),
            pltpu.VMEM((HALF * 8, LANES), F32),
            pltpu.VMEM((RANK, LANES), F32),
            pltpu.VMEM((CL_DEV, RANK, RANK), F32),
            pltpu.VMEM((3, LANES, LANES), BF16),
            pltpu.VMEM((3, RANK + HALF, LANES), F32),
            pltpu.VMEM((GROUP, HALF, LANES), F32),
            pltpu.VMEM((8 * PITCH, LANES), F32),
            pltpu.VMEM((8 * RANK, LANES), F32),
            pltpu.VMEM((8, WIDE), jnp.int32),
            pltpu.VMEM((8, WIDE), jnp.int32),
            pltpu.SMEM((8, WIDE), jnp.int32),
            pltpu.VMEM((ROW_SLOTS, RANK, LANES), BF16),
            pltpu.VMEM((COLUMNS, RANK, LANES), BF16),
            pltpu.VMEM((COLUMNS, RANK, LANES), BF16),
            pltpu.VMEM((blocks + 1, HALF, LANES), BF16),
            pltpu.VMEM((blocks + 1, HALF, LANES), BF16),
            pltpu.VMEM((4 * fours, HALF, LANES), F32),
            pltpu.VMEM((fours + 1, RANK, LANES), F32),
            pltpu.VMEM((SLOTS * HALF, LANES), BF16),
            pltpu.SemaphoreType.DMA((8,)),
            pltpu.SemaphoreType.DMA((blocks // 16 + 1,)),
            pltpu.SemaphoreType.DMA,
            pltpu.SemaphoreType.DMA((count,)),
            pltpu.SemaphoreType.DMA((count,)),
            pltpu.SemaphoreType.DMA((reps - 1,)),
            pltpu.SemaphoreType.DMA((reps - 1,)),
        ],
        compiler_params=pltpu.CompilerParams(
            collective_id=0, has_side_effects=True, vmem_limit_bytes=60 * MIB
        ),
        name="upsweep_and_blocks",
    )(order, bottom, zero, one, two, three, admissible, coupling)


def deliver_kernel(
    parts, projected_in, shares_in, projected_to, zero_to, one_to, two_to,
    projected, shares, total, zero, one, two, came, went,
):
    rows = projected.shape[0] // parts
    spans = [pl.ds(k * rows, rows) for k in range(parts)]
    reads = [
        pltpu.make_async_copy(projected_in.at[span], projected.at[span], came.at[k])
        for k, span in enumerate(spans)
    ]
    writes = [
        pltpu.make_async_copy(projected.at[span], projected_to.at[span], went.at[k])
        for k, span in enumerate(spans)
    ]
    fetch = pltpu.make_async_copy(shares_in, shares, came.at[parts])
    for read in reads[:1] + [fetch] + reads[1:]:
        read.start()
    for read, write in zip(reads, writes):
        read.wait()
        write.start()
    fetch.wait()
    summed = shares[0].astype(F32)
    for k in range(1, shares.shape[0]):
        summed = summed + shares[k].astype(F32)
    for s in range(SLOTS):
        total[s * APART : s * APART + HALF, :] = summed[s * HALF : (s + 1) * HALF]
    for tile in range(HALF):
        span = slice(tile * LANES, (tile + 1) * LANES)
        zero[:, span] = total[pl.ds(tile, CL_DEV, stride=APART), :]
        one[:, span] = total[pl.ds(tile + CL_DEV * APART, CL_DEV // 2, stride=APART), :]
        at = tile + (SLOTS - 1) * APART
        two[:, span] = total[at : at + 1, :]
    for k, (source, target) in enumerate(((zero, zero_to), (one, one_to), (two, two_to))):
        writes.append(pltpu.make_async_copy(source, target, went.at[parts + k]))
        writes[-1].start()
    for write in writes:
        write.wait()


def deliver_call(projected, shares):
    hbm = pl.BlockSpec(memory_space=pltpu.HBM)
    parts = 4
    small = [(count, FLAT) for count in (CL_DEV, CL_DEV // 2, 1)]
    return pl.pallas_call(
        functools.partial(deliver_kernel, parts),
        out_shape=[jax.ShapeDtypeStruct(projected.shape, BF16)]
        + [jax.ShapeDtypeStruct(shape, F32) for shape in small],
        in_specs=[hbm] * 2,
        out_specs=[hbm] * 4,
        scratch_shapes=[
            pltpu.VMEM(projected.shape, BF16),
            pltpu.VMEM(shares.shape, BF16),
            pltpu.VMEM((SLOTS * APART, LANES), F32),
            *[pltpu.VMEM(shape, F32) for shape in small],
            pltpu.SemaphoreType.DMA((parts + 1,)),
            pltpu.SemaphoreType.DMA((parts + 3,)),
        ],
        compiler_params=pltpu.CompilerParams(vmem_limit_bytes=60 * MIB),
        name="deliver",
    )(projected, shares)


def local(leaves, reps, bottom, zero, one, two, three, order, coupling, admissible):
    return tuple(deliver_call(
        *main_call(leaves, reps, order, bottom, zero, one, two, three, admissible, coupling)
    ))


def solution(mesh):
    return jax.shard_map(
        functools.partial(local, mesh.shape["leaf"], mesh.shape["rep"]),
        mesh=mesh,
        in_specs=(
            P("leaf", None),
            P("leaf", None),
            P("leaf", None),
            P("leaf", None),
            P(),
            P("leaf", None),
            P(("leaf", "rep"), None),
            P(None, ("leaf", "rep")),
        ),
        out_specs=(P(("leaf", "rep"), None), P("leaf", None), P("leaf", None), P("leaf", None)),
        check_vma=False,
    )
```
